32 devices in a mesh: seq: 8 (over z, x), batch: 4 (over y, core).
Axes of the slice: x: 2, y: 2, z: 4, core: 2. Of those that a mesh axis runs over, the one named last changes fastest.
Arguments:
- tokens: bfloat16 [4, 4096, 576], P('batch', 'seq'), may hold values from -6 to 6
- segment_ids: int32 [4, 4096], P('batch', 'seq'), may hold values from 0 to 130, as said below
- gain_attn: bfloat16 [576], replicated, may hold values from 0.5 to 1.5
- w_query: bfloat16 [576, 576], replicated, may hold values from -0.5 to 0.5
- w_key: bfloat16 [576, 192], replicated, may hold values from -0.25 to 0.25
- w_value: bfloat16 [576, 192], replicated, may hold values from -0.25 to 0.25
- w_out: bfloat16 [576, 576], replicated, may hold values from -2 to 2
- gain_mlp: bfloat16 [576], replicated, may hold values from 0.5 to 1.5
- w_gate: bfloat16 [576, 1536], replicated, may hold values from -0.25 to 0.25
- w_up: bfloat16 [576, 1536], replicated, may hold values from -0.25 to 0.25
- w_down: bfloat16 [1536, 576], replicated, may hold values from -0.15625 to 0.15625
- cotangent: bfloat16 [4, 4096, 576], P('batch', 'seq'), may hold values from -6 to 6
Outputs:
- output: bfloat16 [4, 4096, 576], P('batch', 'seq')
- tokens_grad: float32 [4, 4096, 576], P('batch', 'seq')
- gain_attn_grad: float32 [576], replicated
- w_query_grad: float32 [576, 576], replicated
- w_key_grad: float32 [576, 192], replicated
- w_value_grad: float32 [576, 192], replicated
- w_out_grad: float32 [576, 576], replicated
- gain_mlp_grad: float32 [576], replicated
- w_gate_grad: float32 [576, 1536], replicated
- w_up_grad: float32 [576, 1536], replicated
- w_down_grad: float32 [1536, 576], replicated
The draws below stay inside these ranges and needn't reach their ends.
Inputs may be any that keep to these rules, and one draw needn't show every extreme that they name: `segment_ids`: along each sequence the ids start at 0, never fall and rise by at most one from token to token; each sequence holds exactly 131 documents; one document of each sequence begins within its first 512 tokens and ends within its last 512.
All inputs are finite; a program needn't handle non-finite values.
Results may differ from the reference program's by a relative error of at most 0.02.
Values may be sent and summed in bfloat16 or wider, within the bound.
A program may use at most 192 MiB of HBM per device.

```python
import jax
import jax.numpy as jnp
from jax import lax

D = 576
H = 9
KVH = 3
HD = 64
FF = 1536
TOK_DEV = 512
SEQS = 4
LEN = 4096


def draw_segment_ids(key, part):
    key = jax.random.fold_in(key, 7)
    key_start, key_finish, key_pick = jax.random.split(key, 3)
    extra = TOK_DEV // 4
    begin_long = jax.random.randint(key_start, (SEQS, 1), TOK_DEV // 2, TOK_DEV)
    end_long = LEN - jax.random.randint(key_finish, (SEQS, 1), TOK_DEV // 2, TOK_DEV)
    index = jnp.arange(LEN, dtype=jnp.int32)[None, :]
    outside = ((index < begin_long) | (index > end_long)) & (index > 0)
    row_keys = jax.random.split(key_pick, SEQS)
    orders = jax.vmap(lambda row_key: jax.random.permutation(row_key, LEN))(row_keys).astype(jnp.int32)
    scores = jnp.where(outside, orders, -1)
    unused, picked = lax.top_k(scores, extra)
    chosen = jnp.any(index[:, None, :] == picked[:, :, None], axis=1)
    fresh = (index == begin_long) | (index == end_long) | chosen
    return jnp.cumsum(fresh.astype(jnp.int32), axis=1).astype(jnp.int32)


def level_of(key, shape, shards, smallest, high):
    def one(position, blocks):
        heights = jax.random.uniform(jax.random.fold_in(jax.random.fold_in(key, 6), position), (blocks,), jnp.float32, smallest / len(shards), high / len(shards))
        return jnp.repeat(jnp.exp(heights), shape[position] // blocks).reshape((-1,) + (1,) * (len(shape) - position - 1))

    loudness = one(*shards[0])
    for cut in shards[1:]:
        loudness = loudness * one(*cut)
    return loudness


def bell_draw(own_key, shape, deviation, limit, cuts=(), held_as=jnp.bfloat16):
    values = deviation * jax.random.normal(own_key, shape, jnp.float32)
    if cuts:
        values = values * level_of(own_key, shape, cuts, -0.22, 0.18)
    return jnp.clip(values, -limit, limit).astype(held_as)


def setup_inputs(seed: int = 0) -> dict:
    keys = jax.random.split(jax.random.key(seed), 13)
    tokens = bell_draw(keys[0], (SEQS, LEN, D), 1.0, 6.0, ((0, 4), (1, 8)))
    segment_ids = draw_segment_ids(jax.random.fold_in(keys[12], 71), 0)
    gain_attn = jnp.clip(1.0 + 0.1 * jax.random.normal(keys[2], (D,), jnp.float32), 0.5, 1.5).astype(jnp.bfloat16)
    w_query = bell_draw(keys[3], (D, H * HD), (D // 4) ** -0.5, 0.5)
    w_key = bell_draw(keys[4], (D, KVH * HD), D ** -0.5, 0.25)
    w_value = bell_draw(keys[5], (D, KVH * HD), D ** -0.5, 0.25)
    w_out = bell_draw(keys[6], (H * HD, D), (max(H * HD // 64, 1)) ** -0.5, 2.0)
    gain_mlp = jnp.clip(1.0 + 0.1 * jax.random.normal(keys[7], (D,), jnp.float32), 0.5, 1.5).astype(jnp.bfloat16)
    w_gate = bell_draw(keys[8], (D, FF), D ** -0.5, 0.25)
    w_up = bell_draw(keys[9], (D, FF), D ** -0.5, 0.25)
    w_down = bell_draw(keys[10], (FF, D), FF ** -0.5, 0.15625)
    cotangent = bell_draw(keys[11], (SEQS, LEN, D), 1.0, 6.0, ((0, 4), (1, 8)))
    return dict(tokens=tokens, segment_ids=segment_ids, gain_attn=gain_attn, w_query=w_query, w_key=w_key, w_value=w_value, w_out=w_out, gain_mlp=gain_mlp, w_gate=w_gate, w_up=w_up, w_down=w_down, cotangent=cotangent)


@jax.custom_vjp
def low(v):
    return lax.optimization_barrier(v.astype(jnp.bfloat16)).astype(jnp.float32)

@jax.custom_vjp
def low_back(v):
    return v

def low_keep(v):
    return (low(v), None)

def low_pass(kept, grad):
    return (grad,)

def back_keep(v):
    return (v, None)

def back_low(kept, grad):
    return (low(grad),)
low.defvjp(low_keep, low_pass)
low_back.defvjp(back_keep, back_low)
epsilon = 1e-05
theta_base = 10000.0
masked_value = -1e+30

def positions(seg_ids):
    length = seg_ids.shape[0]
    index = jnp.arange(length, dtype=jnp.int32)
    fresh = jnp.concatenate([jnp.ones((1,), dtype=jnp.bool_), seg_ids[1:] != seg_ids[:-1]])
    begins = lax.cummax(jnp.where(fresh, index, jnp.zeros_like(index)), axis=0)
    return index - begins

def rotate(vectors, places):
    half = vectors.shape[-1] // 2
    freqs = theta_base ** (-2.0 * jnp.arange(half, dtype=jnp.float32) / vectors.shape[-1])
    angles = places.astype(jnp.float32)[:, None] * freqs[None, :]
    cosine = jnp.cos(angles)[:, None, :]
    sine = jnp.sin(angles)[:, None, :]
    first = vectors[..., :half]
    second = vectors[..., half:]
    return jnp.concatenate([first * cosine - second * sine, second * cosine + first * sine], axis=-1)

def rms_norm(values_in, gain):
    return values_in * lax.rsqrt(lax.optimization_barrier(jnp.mean(values_in * values_in, axis=-1, keepdims=True)) + epsilon) * gain

def layer_forward(inputs, seg_ids, places, gain_attn, w_query, w_key, w_value, w_out, gain_mlp, w_gate, w_up, w_down):
    highest = lax.Precision.HIGHEST
    length = inputs.shape[0]
    group_size = H // KVH
    factor = HD ** (-0.5)
    normed = low(rms_norm(inputs, gain_attn))
    queries = low(rotate(low_back(jnp.dot(normed, w_query, precision=highest)).reshape(length, H, HD), places))
    keys_rot = low(rotate(low_back(jnp.dot(normed, w_key, precision=highest)).reshape(length, KVH, HD), places))
    values_all = low(low_back(jnp.dot(normed, w_value, precision=highest))).reshape(length, KVH, HD)
    block_rows = 512 if length % 512 == 0 else length
    count_blocks = length // block_rows
    query_blocks = queries.reshape(count_blocks, block_rows, KVH, group_size, HD)
    block_starts = block_rows * jnp.arange(count_blocks, dtype=jnp.int32)
    key_index = jnp.arange(length, dtype=jnp.int32)

    def attend(pair):
        query_block, block_start = pair
        raw_scores = jnp.einsum('qkgd,jkd->kgqj', query_block, keys_rot, precision=highest)
        scores = factor * low_back(raw_scores)
        query_seg = lax.dynamic_slice_in_dim(seg_ids, block_start, block_rows)
        query_index = block_start + jnp.arange(block_rows, dtype=jnp.int32)
        visible = (query_seg[:, None] == seg_ids[None, :]) & (query_index[:, None] >= key_index[None, :])
        scores = jnp.where(visible, scores, masked_value)
        probs = low(jax.nn.softmax(scores, axis=-1))
        return jnp.einsum('kgqj,jkd->qkgd', probs, values_all, precision=highest)
    attended = lax.map(jax.checkpoint(attend), (query_blocks, block_starts))
    attended = low(low_back(attended.reshape(length, H * HD)))
    middle = inputs + low_back(jnp.dot(attended, w_out, precision=highest))
    normed_mlp = low(rms_norm(middle, gain_mlp))
    gate = low_back(jnp.dot(normed_mlp, w_gate, precision=highest))
    up_proj = low_back(jnp.dot(normed_mlp, w_up, precision=highest))
    hidden = low(jax.nn.silu(gate) * up_proj)
    return middle + low_back(jnp.dot(hidden, w_down, precision=highest))

def reference(tokens, segment_ids, gain_attn, w_query, w_key, w_value, w_out, gain_mlp, w_gate, w_up, w_down, cotangent):
    weights = tuple((entry.astype(jnp.float32) for entry in (gain_attn, w_query, w_key, w_value, w_out, gain_mlp, w_gate, w_up, w_down)))

    def one_sequence(totals, batch_item):
        tokens_seq, seg_ids, cot_seq = batch_item
        places = positions(seg_ids)

        def forward(inputs, *params):
            return layer_forward(inputs, seg_ids, places, *params)
        result, pullback = jax.vjp(forward, tokens_seq.astype(jnp.float32), *weights)
        grads = pullback(cot_seq.astype(jnp.float32))
        totals = jax.tree.map(jnp.add, totals, tuple(grads[1:]))
        return (totals, (result.astype(jnp.bfloat16), grads[0]))
    zeros_init = tuple((jnp.zeros_like(entry) for entry in weights))
    totals, (outputs, tokens_grad) = lax.scan(one_sequence, zeros_init, (tokens, segment_ids, cotangent))
    return (outputs, tokens_grad, totals[0], totals[1], totals[2], totals[3], totals[4], totals[5], totals[6], totals[7], totals[8])
```

```python
import functools

import jax
import jax.numpy as jnp
import numpy as np
from jax import lax
from jax.experimental import pallas as pl
from jax.experimental.pallas import tpu as pltpu
from jax.sharding import PartitionSpec as P

H = 9
KVH = 3
HD = 64
GROUP = H // KVH
PAIR = 2 * HD
META = 16

epsilon = 1e-05
theta_base = 10000.0
masked_value = -1e30
never = 1e30
LOG2E = 1.4426950408889634
LN2 = 0.6931471805599453
MESH = pl.DeviceIdType.MESH
f32 = jnp.float32
bf16 = jnp.bfloat16
VMEM_LIMIT = 60 * 2**20


def dot(left, right, left_dim, right_dim):
    return lax.dot_general(
        left,
        right,
        (((left_dim,), (right_dim,)), ((), ())),
        preferred_element_type=f32,
    )


def angle_table(ranks, rows):
    half = HD // 2
    freqs = theta_base ** (-2.0 * np.arange(half, dtype=np.float64) / HD)
    angles = freqs[:, None] * np.arange(ranks * rows, dtype=np.float64)[None, :]
    table = np.concatenate([np.cos(angles), np.sin(angles)], axis=0).astype(np.float32)
    return np.ascontiguousarray(table.reshape(HD, ranks, rows).transpose(1, 0, 2))


def turn(vectors, cosine, sine):
    half = HD // 2
    first, second = vectors[:half], vectors[half:]
    return jnp.concatenate(
        [first * cosine - second * sine, second * cosine + first * sine], axis=0
    )


def turn_back(vectors, cosine, sine):
    half = HD // 2
    first, second = vectors[:half], vectors[half:]
    return jnp.concatenate(
        [first * cosine + second * sine, second * cosine - first * sine], axis=0
    )


def own_bias(seg_row):
    rows = seg_row.shape[1]
    ids = seg_row.astype(f32)
    columns = jnp.broadcast_to(ids, (128, rows)).T[:, :1]
    key = lax.broadcasted_iota(jnp.int32, (rows, rows), 0)
    query = lax.broadcasted_iota(jnp.int32, (rows, rows), 1)
    visible = (columns == ids) & (key <= query)
    return jnp.where(visible, 0.0, masked_value)


def long_row(seg_row):
    return seg_row == seg_row[:, :1]


def first_bias(meta, rows):
    start = 2.0 * meta[0:1, :1].astype(f32) + meta[1:2, :1].astype(f32)
    key = lax.broadcasted_iota(jnp.int32, (rows, 1), 0).astype(f32)
    return jnp.where(key >= start, 0.0, masked_value)


def attend_kernel(
    ranks,
    tokens_ref,
    seg_ref,
    gain_ref,
    wq_ref,
    wk_ref,
    wv_ref,
    table_ref,
    qt_ref,
    kv_ref,
    att_ref,
    lse_ref,
    turn_ref,
    max_ref,
    sum_ref,
    turn_sem,
    z_sem,
    x_sem,
    in_sem,
):
    rank = lax.axis_index("seq")
    row = lax.axis_index("batch")
    rows = tokens_ref.shape[0]
    depth = lax.div(rank, 2)
    odd = lax.rem(rank, 2)
    mate = rank + 1 - 2 * odd
    has_up = rank + 2 < ranks
    has_down = rank >= 2

    turn_copy = pltpu.make_async_copy(table_ref.at[rank], turn_ref, turn_sem)
    turn_copy.start()

    barrier = pltpu.get_barrier_semaphore()
    pl.semaphore_signal(barrier, inc=1, device_id=(mate, row), device_id_type=MESH)

    @pl.when(has_up)
    def _():
        pl.semaphore_signal(barrier, inc=1, device_id=(rank + 2, row), device_id_type=MESH)

    @pl.when(has_down)
    def _():
        pl.semaphore_signal(barrier, inc=1, device_id=(rank - 2, row), device_id_type=MESH)

    def z_copy(block, group):
        return pltpu.make_async_remote_copy(
            src_ref=kv_ref.at[block, group],
            dst_ref=kv_ref.at[block, group],
            send_sem=z_sem.at[block, group],
            recv_sem=in_sem.at[block, group],
            device_id=(rank + 2, row),
            device_id_type=MESH,
        )

    def x_copy(block, group):
        return pltpu.make_async_remote_copy(
            src_ref=kv_ref.at[block, group],
            dst_ref=kv_ref.at[block, group],
            send_sem=x_sem.at[block, group],
            recv_sem=in_sem.at[block, group],
            device_id=(mate, row),
            device_id_type=MESH,
        )

    inputs = tokens_ref[...].astype(f32)
    inverse = lax.rsqrt(jnp.mean(inputs * inputs, axis=-1, keepdims=True) + epsilon)
    normed = (inputs * inverse * gain_ref[...].astype(f32)).astype(bf16)
    keys = dot(wk_ref[...], normed, 0, 1)
    values = dot(wv_ref[...], normed, 0, 1)
    seg_row = seg_ref[...]
    start = jnp.sum((seg_row != seg_row[:, rows - 1 :]).astype(f32), axis=1, keepdims=True)
    high = jnp.floor(0.5 * start)
    low = start - 2.0 * high
    which = lax.broadcasted_iota(jnp.int32, (META, PAIR), 0)
    meta = jnp.where(which == 0, high, jnp.where(which == 1, low, 0.0)).astype(bf16)
    turn_copy.wait()
    cosine = turn_ref[: HD // 2]
    sine = turn_ref[HD // 2 :]
    for group in range(KVH):
        part = slice(group * HD, group * HD + HD)
        both = jnp.concatenate([turn(keys[part], cosine, sine), values[part]], axis=0)
        kv_ref[rank, group, :rows, :] = both.astype(bf16).T
        kv_ref[rank, group, rows:, :] = meta

    pl.semaphore_wait(barrier, 1 + has_up.astype(jnp.int32) + has_down.astype(jnp.int32))
    for group in range(KVH):

        @pl.when(odd == 0)
        def _():
            x_copy(rank, group).start()

        @pl.when(has_up)
        def _():
            z_copy(rank, group).start()

    def relay(level, group):
        block = rank - 2 * level
        z_in = pltpu.make_async_remote_copy(
            src_ref=kv_ref.at[block, group],
            dst_ref=kv_ref.at[block, group],
            send_sem=z_sem.at[block, group],
            recv_sem=in_sem.at[block, group],
            device_id=(mate, row),
            device_id_type=MESH,
        )
        z_in.wait_recv()
        x_copy(block, group).start()

        @pl.when(has_up)
        def _():
            z_copy(block, group).start()

    queries = dot(wq_ref[...], normed, 0, 1)
    for head in range(H):
        part = slice(head * HD, head * HD + HD)
        turned = turn(queries[part], cosine, sine) * (LOG2E / HD**0.5)
        qt_ref[head, :HD, :] = turned.astype(bf16)
        qt_ref[head, HD:, :] = jnp.zeros((HD, rows), bf16)

    bias = own_bias(seg_row)
    for group in range(KVH):
        pair = kv_ref[rank, group, :rows, :]
        values_t = pair.T[HD:]
        for head in range(group * GROUP, (group + 1) * GROUP):
            scores = dot(pair, qt_ref[head], 1, 0) + bias
            top = jnp.max(scores, axis=0, keepdims=True)
            weights = jnp.exp2(scores - top)
            max_ref[head : head + 1, :] = top
            sum_ref[head : head + 1, :] = jnp.sum(weights, axis=0, keepdims=True)
            att_ref[head * HD : (head + 1) * HD, :] = dot(values_t, weights.astype(bf16), 1, 0)

        @pl.when(depth >= 1)
        def _():
            relay(1, group)

    in_long = long_row(seg_row)

    def block_step(block, group, key_bias):
        pair = kv_ref[block, group, :rows, :]
        values_t = pair.T[HD:]
        heads = range(group * GROUP, (group + 1) * GROUP)
        old_max = [max_ref[head : head + 1, :] for head in heads]
        old_sum = [sum_ref[head : head + 1, :] for head in heads]
        old_att = [att_ref[head * HD : (head + 1) * HD, :] for head in heads]
        results = []
        for spot, head in enumerate(heads):
            scores = dot(pair, qt_ref[head], 1, 0)
            if key_bias is not None:
                scores = scores + key_bias
            top = jnp.maximum(old_max[spot], jnp.max(scores, axis=0, keepdims=True))
            top = jnp.where(in_long, top, old_max[spot])
            weights = jnp.exp2(scores - jnp.where(in_long, top, never))
            scale = jnp.exp2(old_max[spot] - top)
            results.append(
                (
                    top,
                    old_sum[spot] * scale + jnp.sum(weights, axis=0, keepdims=True),
                    old_att[spot] * scale + dot(values_t, weights.astype(bf16), 1, 0),
                )
            )
        for spot, head in enumerate(heads):
            max_ref[head : head + 1, :] = results[spot][0]
            sum_ref[head : head + 1, :] = results[spot][1]
            att_ref[head * HD : (head + 1) * HD, :] = results[spot][2]

    def step(index, carry):
        level = lax.div(index + 1, 2)
        straight = lax.rem(index, 2) == 1
        block = jnp.where(straight, rank, mate) - 2 * level
        for group in range(KVH):

            @pl.when(straight & (level + 1 <= depth))
            def _():
                relay(level + 1, group)

            @pl.when(jnp.logical_not(straight))
            def _():
                x_copy(block, group).wait_recv()

            @pl.when(block == 0)
            def _():
                key_bias = first_bias(kv_ref[0, group, rows:, :], rows)
                block_step(block, group, key_bias)

            @pl.when(block != 0)
            def _():
                block_step(block, group, None)

        return carry

    lax.fori_loop(1 - odd, 2 * depth + 1, step, 0)

    for head in range(H):
        part = slice(head * HD, (head + 1) * HD)
        total = sum_ref[head : head + 1, :]
        att_ref[part, :] = att_ref[part, :] / total
        lse_ref[head : head + 1, :] = max_ref[head : head + 1, :] + jnp.log2(total)
    lse_ref[H:, :] = jnp.zeros_like(lse_ref[H:, :])

    def sent(level, carry):
        block = rank - 2 * level
        for group in range(KVH):

            @pl.when(has_up)
            def _():
                z_copy(block, group).wait_send()

            @pl.when((odd == 0) | (level >= 1))
            def _():
                x_copy(block, group).wait_send()

        return carry

    lax.fori_loop(0, depth + 1, sent, 0)


def attend(tokens, seg_row, gain, wq, wk, wv, ranks):
    rows, width = tokens.shape
    vmem = pl.BlockSpec(memory_space=pltpu.VMEM)
    table = jnp.asarray(angle_table(ranks, rows))
    dma = pltpu.SemaphoreType.DMA
    return pl.pallas_call(
        functools.partial(attend_kernel, ranks),
        out_shape=(
            jax.ShapeDtypeStruct((H, PAIR, rows), bf16),
            jax.ShapeDtypeStruct((ranks, KVH, rows + META, PAIR), bf16),
            jax.ShapeDtypeStruct((H * HD, rows), f32),
            jax.ShapeDtypeStruct((16, rows), f32),
        ),
        in_specs=[vmem] * 6 + [pl.BlockSpec(memory_space=pl.ANY)],
        out_specs=(vmem,) * 4,
        scratch_shapes=[
            pltpu.VMEM((HD, rows), f32),
            pltpu.VMEM((16, rows), f32),
            pltpu.VMEM((16, rows), f32),
            dma(()),
            dma((ranks, KVH)),
            dma((ranks, KVH)),
            dma((ranks, KVH)),
        ],
        compiler_params=pltpu.CompilerParams(
            collective_id=0, has_side_effects=True, vmem_limit_bytes=VMEM_LIMIT
        ),
        name="attend",
    )(tokens, seg_row, gain, wq, wk, wv, table)


def mlp_kernel(
    tokens_ref,
    cot_ref,
    att_ref,
    w_out_ref,
    gain_ref,
    w_gate_ref,
    w_up_ref,
    w_down_ref,
    out_ref,
    grads_ref,
    grad_out_ref,
    gain_grad_ref,
    d_middle_ref,
    dot_ref,
    delta_ref,
):
    rows, width = tokens_ref.shape
    hidden_units = w_gate_ref.shape[1]
    chunk = 512
    inputs = tokens_ref[...].astype(f32)
    attended = att_ref[...].astype(bf16).T
    middle = inputs + dot(attended, w_out_ref[...], 1, 0)
    inverse = lax.rsqrt(jnp.mean(middle * middle, axis=-1, keepdims=True) + epsilon)
    scaled = middle * inverse
    gain = gain_ref[...].astype(f32)
    normed = (scaled * gain).astype(bf16)
    normed_t = normed.T
    cot = cot_ref[...]
    cot_t = cot.T
    result = middle
    d_normed = jnp.zeros((rows, width), f32)
    for first in range(0, hidden_units, chunk):
        part = slice(first, first + chunk)
        gate = dot(normed, w_gate_ref[:, part], 1, 0)
        up = dot(normed, w_up_ref[:, part], 1, 0)
        d_hidden = dot(cot, w_down_ref[part, :], 1, 1)
        sigmoid = jax.nn.sigmoid(gate)
        silu = gate * sigmoid
        hidden = (silu * up).astype(bf16)
        d_gate = (d_hidden * up * (sigmoid + silu * (1.0 - sigmoid))).astype(bf16)
        d_up = (d_hidden * silu).astype(bf16)
        result = result + dot(hidden, w_down_ref[part, :], 1, 0)
        d_normed = d_normed + dot(d_gate, w_gate_ref[:, part], 1, 1)
        d_normed = d_normed + dot(d_up, w_up_ref[:, part], 1, 1)
        grads_ref[0, :, part] = dot(normed_t, d_gate, 1, 0).astype(bf16)
        grads_ref[1, :, part] = dot(normed_t, d_up, 1, 0).astype(bf16)
        grads_ref[2, :, part] = dot(cot_t, hidden, 1, 0).astype(bf16)
    out_ref[...] = result.astype(bf16)
    gain_grad_ref[...] = jnp.sum(d_normed * scaled, axis=0, keepdims=True)
    mixed = d_normed * gain
    d_middle = cot.astype(f32) + inverse * (
        mixed - scaled * jnp.mean(mixed * scaled, axis=-1, keepdims=True)
    )
    d_middle_ref[...] = d_middle
    d_branch = d_middle.astype(bf16)
    grad_out_ref[...] = dot(att_ref[...].astype(bf16), d_branch, 1, 0).astype(bf16)
    d_attended = dot(w_out_ref[...], d_branch, 1, 1).astype(bf16)
    for head in range(H):
        part = slice(head * HD, (head + 1) * HD)
        dot_ref[head, :HD, :] = jnp.zeros((HD, rows), bf16)
        dot_ref[head, HD:, :] = d_attended[part]
        delta_ref[head : head + 1, :] = jnp.sum(
            d_attended[part].astype(f32) * att_ref[part, :], axis=0, keepdims=True
        )
    delta_ref[H:, :] = jnp.zeros_like(delta_ref[H:, :])


def mlp(tokens, cot, att, w_out, gain, w_gate, w_up, w_down):
    rows, width = tokens.shape
    hidden_units = w_gate.shape[1]
    vmem = pl.BlockSpec(memory_space=pltpu.VMEM)
    return pl.pallas_call(
        mlp_kernel,
        out_shape=(
            jax.ShapeDtypeStruct((rows, width), bf16),
            jax.ShapeDtypeStruct((3, width, hidden_units), bf16),
            jax.ShapeDtypeStruct((H * HD, width), bf16),
            jax.ShapeDtypeStruct((1, width), f32),
            jax.ShapeDtypeStruct((rows, width), f32),
            jax.ShapeDtypeStruct((H, PAIR, rows), bf16),
            jax.ShapeDtypeStruct((16, rows), f32),
        ),
        in_specs=[vmem] * 8,
        out_specs=(vmem,) * 7,
        compiler_params=pltpu.CompilerParams(vmem_limit_bytes=VMEM_LIMIT),
        name="mlp",
    )(tokens, cot, att, w_out, gain, w_gate, w_up, w_down)


def back_kernel(
    ranks,
    seg_ref,
    turn_ref,
    qt_ref,
    kv_ref,
    lse_ref,
    dot_ref,
    delta_ref,
    terms_ref,
    dq_ref,
    acc_ref,
):
    rank = lax.axis_index("seq")
    rows = seg_ref.shape[1]
    seg_row = seg_ref[...]
    in_long = long_row(seg_row)
    acc_ref[...] = jnp.zeros_like(acc_ref)

    def pair_step(block, group, bias, level_of):
        pair = kv_ref[block, group, :rows, :]
        keys_t = pair.T[:HD]
        heads = range(group * GROUP, (group + 1) * GROUP)
        old = [acc_ref[head] for head in heads]
        total = jnp.zeros((rows, PAIR), f32)
        results = []
        for spot, head in enumerate(heads):
            scores = dot(pair, qt_ref[head], 1, 0)
            if bias is not None:
                scores = scores + bias
            probs = jnp.exp2(scores - level_of(lse_ref[head : head + 1, :]))
            d_probs = dot(pair, dot_ref[head], 1, 0)
            d_scores = (probs * (d_probs - delta_ref[head : head + 1, :])).astype(bf16)
            total = total + dot(probs.astype(bf16), dot_ref[head], 1, 1)
            total = total + dot(d_scores, qt_ref[head], 1, 1)
            results.append(old[spot] + dot(keys_t, d_scores, 1, 0))
        for spot, head in enumerate(heads):
            acc_ref[head] = results[spot]
        terms_ref[block, group] = total.astype(bf16)

    def level_off(lse):
        return jnp.where(in_long, lse, never)

    def step(block, carry):
        @pl.when(block == 0)
        def _():
            for group in range(KVH):
                key_bias = first_bias(kv_ref[0, group, rows:, :], rows)
                pair_step(block, group, key_bias, level_off)

        @pl.when(block != 0)
        def _():
            for group in range(KVH):
                pair_step(block, group, None, level_off)

        return carry

    lax.fori_loop(0, rank, step, 0)
    bias = own_bias(seg_row)
    for group in range(KVH):
        pair_step(rank, group, bias, lambda lse: lse)

    def clear(block, carry):
        terms_ref[block] = jnp.zeros((KVH, rows, PAIR), bf16)
        return carry

    lax.fori_loop(rank + 1, ranks, clear, 0)
    cosine = turn_ref[: HD // 2]
    sine = turn_ref[HD // 2 :]
    for head in range(H):
        part = slice(head * HD, (head + 1) * HD)
        dq_ref[part, :] = turn_back(acc_ref[head] * HD**-0.5, cosine, sine).astype(bf16)


def back(seg_row, turn_table, qt, kv, lse, dot_t, delta, ranks):
    rows = seg_row.shape[1]
    vmem = pl.BlockSpec(memory_space=pltpu.VMEM)
    return pl.pallas_call(
        functools.partial(back_kernel, ranks),
        out_shape=(
            jax.ShapeDtypeStruct((ranks, KVH, rows, PAIR), bf16),
            jax.ShapeDtypeStruct((H * HD, rows), bf16),
        ),
        in_specs=[vmem] * 7,
        out_specs=(vmem,) * 2,
        scratch_shapes=[pltpu.VMEM((H, HD, rows), f32)],
        compiler_params=pltpu.CompilerParams(vmem_limit_bytes=VMEM_LIMIT),
        name="back",
    )(seg_row, turn_table, qt, kv, lse, dot_t, delta)


def last_kernel(
    tokens_ref,
    gain_ref,
    wq_ref,
    wk_ref,
    wv_ref,
    turn_ref,
    dq_ref,
    own_ref,
    d_middle_ref,
    out_ref,
    grads_ref,
    gain_grad_ref,
    dk_ref,
    dv_ref,
):
    cosine = turn_ref[: HD // 2]
    sine = turn_ref[HD // 2 :]
    for group in range(KVH):
        part = slice(group * HD, (group + 1) * HD)
        both = own_ref[group].astype(f32).T
        dk_ref[part, :] = turn_back(both[:HD] * LN2, cosine, sine).astype(bf16)
        dv_ref[part, :] = both[HD:].astype(bf16)
    inputs = tokens_ref[...].astype(f32)
    inverse = lax.rsqrt(jnp.mean(inputs * inputs, axis=-1, keepdims=True) + epsilon)
    scaled = inputs * inverse
    gain = gain_ref[...].astype(f32)
    normed_t = (scaled * gain).astype(bf16).T
    q_cols = H * HD
    k_cols = KVH * HD
    grads_ref[:, :q_cols] = dot(normed_t, dq_ref[...], 1, 1).astype(bf16)
    grads_ref[:, q_cols : q_cols + k_cols] = dot(normed_t, dk_ref[...], 1, 1).astype(bf16)
    grads_ref[:, q_cols + k_cols :] = dot(normed_t, dv_ref[...], 1, 1).astype(bf16)
    d_normed = (
        dot(dq_ref[...], wq_ref[...], 0, 1)
        + dot(dk_ref[...], wk_ref[...], 0, 1)
        + dot(dv_ref[...], wv_ref[...], 0, 1)
    )
    gain_grad_ref[...] = jnp.sum(d_normed * scaled, axis=0, keepdims=True)
    mixed = d_normed * gain
    out_ref[...] = d_middle_ref[...] + inverse * (
        mixed - scaled * jnp.mean(mixed * scaled, axis=-1, keepdims=True)
    )


def last(tokens, gain, wq, wk, wv, turn_table, dq, own, d_middle):
    rows, width = tokens.shape
    vmem = pl.BlockSpec(memory_space=pltpu.VMEM)
    return pl.pallas_call(
        last_kernel,
        out_shape=(
            jax.ShapeDtypeStruct((rows, width), f32),
            jax.ShapeDtypeStruct((width, (H + 2 * KVH) * HD), bf16),
            jax.ShapeDtypeStruct((1, width), f32),
        ),
        in_specs=[vmem] * 9,
        out_specs=(vmem,) * 3,
        scratch_shapes=[
            pltpu.VMEM((KVH * HD, rows), bf16),
            pltpu.VMEM((KVH * HD, rows), bf16),
        ],
        compiler_params=pltpu.CompilerParams(vmem_limit_bytes=VMEM_LIMIT),
        name="last",
    )(tokens, gain, wq, wk, wv, turn_table, dq, own, d_middle)


def local(
    ranks,
    tokens,
    segment_ids,
    gain_attn,
    w_query,
    w_key,
    w_value,
    w_out,
    gain_mlp,
    w_gate,
    w_up,
    w_down,
    cotangent,
):
    rows, width = tokens.shape[1:]
    rank = lax.axis_index("seq")
    both_axes = ("seq", "batch")
    gain_first = gain_attn.reshape(1, width)
    gain_second = gain_mlp.reshape(1, width)
    qt, kv, att, lse = attend(
        tokens[0], segment_ids, gain_first, w_query, w_key, w_value, ranks
    )
    output, grads, grad_out, grad_gain_mlp, d_middle, dot_t, delta = mlp(
        tokens[0], cotangent[0], att, w_out, gain_second, w_gate, w_up, w_down
    )
    grads, grad_out = lax.psum((grads, grad_out), both_axes)
    turn_table = lax.dynamic_index_in_dim(
        jnp.asarray(angle_table(ranks, rows)), rank, keepdims=False
    )
    terms, dq = back(segment_ids, turn_table, qt, kv, lse, dot_t, delta, ranks)
    own = lax.psum_scatter(terms, "seq", scatter_dimension=0, tiled=True)[0]
    d_inputs, late, grad_gain_attn = last(
        tokens[0], gain_first, w_query, w_key, w_value, turn_table, dq, own, d_middle
    )
    late = lax.psum(late, both_axes)
    grad_gain_attn, grad_gain_mlp = lax.psum((grad_gain_attn, grad_gain_mlp), both_axes)
    q_cols = H * HD
    k_cols = KVH * HD
    return (
        output[None],
        d_inputs[None],
        grad_gain_attn[0],
        late[:, :q_cols].astype(f32),
        late[:, q_cols : q_cols + k_cols].astype(f32),
        late[:, q_cols + k_cols :].astype(f32),
        grad_out.astype(f32),
        grad_gain_mlp[0],
        grads[0].astype(f32),
        grads[1].astype(f32),
        grads[2].T.astype(f32),
    )


def solution(mesh):
    split = P("batch", "seq", None)
    return jax.shard_map(
        functools.partial(local, mesh.shape["seq"]),
        mesh=mesh,
        in_specs=(split, P("batch", "seq")) + (P(),) * 9 + (split,),
        out_specs=(split, split) + (P(),) * 9,
        check_vma=False,
    )
```

```python
import functools

import jax
import jax.numpy as jnp
import numpy as np
from jax import lax
from jax.experimental import pallas as pl
from jax.experimental.pallas import tpu as pltpu
from jax.sharding import PartitionSpec as P

H = 9
KVH = 3
HD = 64
GROUP = H // KVH
PAIR = 2 * HD
META = 16
LANES = 128
TILES = 4
EXTRA = 64
SPACING = 2

epsilon = 1e-05
theta_base = 10000.0
masked_value = -1e30
never = 1e30
LOG2E = 1.4426950408889634
LN2 = 0.6931471805599453
MESH = pl.DeviceIdType.MESH
f32 = jnp.float32
bf16 = jnp.bfloat16
VMEM_LIMIT = 60 * 2**20


def dot(left, right, left_dim, right_dim):
    return lax.dot_general(
        left,
        right,
        (((left_dim,), (right_dim,)), ((), ())),
        preferred_element_type=f32,
    )


def angle_table(ranks, rows):
    half = HD // 2
    freqs = theta_base ** (-2.0 * np.arange(half, dtype=np.float64) / HD)
    angles = freqs[:, None] * np.arange(ranks * rows, dtype=np.float64)[None, :]
    table = np.concatenate([np.cos(angles), np.sin(angles)], axis=0).astype(np.float32)
    return np.ascontiguousarray(table.reshape(HD, ranks, rows).transpose(1, 0, 2))


def turn(vectors, cosine, sine):
    half = HD // 2
    first, second = vectors[:half], vectors[half:]
    return jnp.concatenate(
        [first * cosine - second * sine, second * cosine + first * sine], axis=0
    )


def turn_back(vectors, cosine, sine):
    half = HD // 2
    first, second = vectors[:half], vectors[half:]
    return jnp.concatenate(
        [first * cosine + second * sine, second * cosine - first * sine], axis=0
    )


def own_bias(seg_row):
    rows = seg_row.shape[1]
    ids = seg_row.astype(f32)
    columns = jnp.broadcast_to(ids, (128, rows)).T[:, :1]
    key = lax.broadcasted_iota(jnp.int32, (rows, rows), 0)
    query = lax.broadcasted_iota(jnp.int32, (rows, rows), 1)
    visible = (columns == ids) & (key <= query)
    return jnp.where(visible, 0.0, masked_value)


def long_row(seg_row):
    return seg_row == seg_row[:, :1]


def first_bias(meta, rows):
    start = 2.0 * meta[0:1, :1].astype(f32) + meta[1:2, :1].astype(f32)
    key = lax.broadcasted_iota(jnp.int32, (rows, 1), 0).astype(f32)
    return jnp.where(key >= start, 0.0, masked_value)


def attend_kernel(
    ranks,
    tokens_ref,
    seg_ref,
    gain_ref,
    wq_ref,
    wk_ref,
    wv_ref,
    table_ref,
    qt_ref,
    kv_ref,
    att_ref,
    lse_ref,
    turn_ref,
    max_ref,
    sum_ref,
    turn_sem,
    z_sem,
    x_sem,
    in_sem,
):
    rank = lax.axis_index("seq")
    row = lax.axis_index("batch")
    rows = tokens_ref.shape[0]
    depth = lax.div(rank, 2)
    odd = lax.rem(rank, 2)
    mate = rank + 1 - 2 * odd
    has_up = rank + 2 < ranks
    has_down = rank >= 2

    turn_copy = pltpu.make_async_copy(table_ref.at[rank], turn_ref, turn_sem)
    turn_copy.start()

    barrier = pltpu.get_barrier_semaphore()
    pl.semaphore_signal(barrier, inc=1, device_id=(mate, row), device_id_type=MESH)

    @pl.when(has_up)
    def _():
        pl.semaphore_signal(barrier, inc=1, device_id=(rank + 2, row), device_id_type=MESH)

    @pl.when(has_down)
    def _():
        pl.semaphore_signal(barrier, inc=1, device_id=(rank - 2, row), device_id_type=MESH)

    def z_copy(block, group):
        return pltpu.make_async_remote_copy(
            src_ref=kv_ref.at[block, group],
            dst_ref=kv_ref.at[block, group],
            send_sem=z_sem.at[block, group],
            recv_sem=in_sem.at[block, group],
            device_id=(rank + 2, row),
            device_id_type=MESH,
        )

    def x_copy(block, group):
        return pltpu.make_async_remote_copy(
            src_ref=kv_ref.at[block, group],
            dst_ref=kv_ref.at[block, group],
            send_sem=x_sem.at[block, group],
            recv_sem=in_sem.at[block, group],
            device_id=(mate, row),
            device_id_type=MESH,
        )

    inputs = tokens_ref[...].astype(f32)
    inverse = lax.rsqrt(jnp.mean(inputs * inputs, axis=-1, keepdims=True) + epsilon)
    normed = (inputs * inverse * gain_ref[...].astype(f32)).astype(bf16)
    keys = dot(wk_ref[...], normed, 0, 1)
    values = dot(wv_ref[...], normed, 0, 1)
    seg_row = seg_ref[...]
    start = jnp.sum((seg_row != seg_row[:, rows - 1 :]).astype(f32), axis=1, keepdims=True)
    high = jnp.floor(0.5 * start)
    low = start - 2.0 * high
    which = lax.broadcasted_iota(jnp.int32, (META, PAIR), 0)
    meta = jnp.where(which == 0, high, jnp.where(which == 1, low, 0.0)).astype(bf16)
    turn_copy.wait()
    cosine = turn_ref[: HD // 2]
    sine = turn_ref[HD // 2 :]
    for group in range(KVH):
        part = slice(group * HD, group * HD + HD)
        both = jnp.concatenate([turn(keys[part], cosine, sine), values[part]], axis=0)
        kv_ref[rank, group, :rows, :] = both.astype(bf16).T
        kv_ref[rank, group, rows:, :] = meta

    pl.semaphore_wait(barrier, 1 + has_up.astype(jnp.int32) + has_down.astype(jnp.int32))
    for group in range(KVH):

        @pl.when(odd == 0)
        def _():
            x_copy(rank, group).start()

        @pl.when(has_up)
        def _():
            z_copy(rank, group).start()

    def relay(level, group):
        block = rank - 2 * level
        z_in = pltpu.make_async_remote_copy(
            src_ref=kv_ref.at[block, group],
            dst_ref=kv_ref.at[block, group],
            send_sem=z_sem.at[block, group],
            recv_sem=in_sem.at[block, group],
            device_id=(mate, row),
            device_id_type=MESH,
        )
        z_in.wait_recv()
        x_copy(block, group).start()

        @pl.when(has_up)
        def _():
            z_copy(block, group).start()

    queries = dot(wq_ref[...], normed, 0, 1)
    for head in range(H):
        part = slice(head * HD, head * HD + HD)
        turned = turn(queries[part], cosine, sine) * (LOG2E / HD**0.5)
        qt_ref[head, :HD, :] = turned.astype(bf16)
        qt_ref[head, HD:, :] = jnp.zeros((HD, rows), bf16)

    bias = own_bias(seg_row)
    for group in range(KVH):
        pair = kv_ref[rank, group, :rows, :]
        values_t = pair.T[HD:]
        for head in range(group * GROUP, (group + 1) * GROUP):
            scores = dot(pair, qt_ref[head], 1, 0) + bias
            top = jnp.max(scores, axis=0, keepdims=True)
            weights = jnp.exp2(scores - top)
            max_ref[head : head + 1, :] = top
            sum_ref[head : head + 1, :] = jnp.sum(weights, axis=0, keepdims=True)
            att_ref[head * HD : (head + 1) * HD, :] = dot(values_t, weights.astype(bf16), 1, 0)

        @pl.when(depth >= 1)
        def _():
            relay(1, group)

    in_long = long_row(seg_row)

    def block_step(block, group, key_bias):
        pair = kv_ref[block, group, :rows, :]
        values_t = pair.T[HD:]
        heads = range(group * GROUP, (group + 1) * GROUP)
        old_max = [max_ref[head : head + 1, :] for head in heads]
        old_sum = [sum_ref[head : head + 1, :] for head in heads]
        old_att = [att_ref[head * HD : (head + 1) * HD, :] for head in heads]
        results = []
        for spot, head in enumerate(heads):
            scores = dot(pair, qt_ref[head], 1, 0)
            if key_bias is not None:
                scores = scores + key_bias
            top = jnp.maximum(old_max[spot], jnp.max(scores, axis=0, keepdims=True))
            top = jnp.where(in_long, top, old_max[spot])
            weights = jnp.exp2(scores - jnp.where(in_long, top, never))
            scale = jnp.exp2(old_max[spot] - top)
            results.append(
                (
                    top,
                    old_sum[spot] * scale + jnp.sum(weights, axis=0, keepdims=True),
                    old_att[spot] * scale + dot(values_t, weights.astype(bf16), 1, 0),
                )
            )
        for spot, head in enumerate(heads):
            max_ref[head : head + 1, :] = results[spot][0]
            sum_ref[head : head + 1, :] = results[spot][1]
            att_ref[head * HD : (head + 1) * HD, :] = results[spot][2]

    def step(index, carry):
        level = lax.div(index + 1, 2)
        straight = lax.rem(index, 2) == 1
        block = jnp.where(straight, rank, mate) - 2 * level
        for group in range(KVH):

            @pl.when(straight & (level + 1 <= depth))
            def _():
                relay(level + 1, group)

            @pl.when(jnp.logical_not(straight))
            def _():
                x_copy(block, group).wait_recv()

            @pl.when(block == 0)
            def _():
                key_bias = first_bias(kv_ref[0, group, rows:, :], rows)
                block_step(block, group, key_bias)

            @pl.when(block != 0)
            def _():
                block_step(block, group, None)

        return carry

    lax.fori_loop(1 - odd, 2 * depth + 1, step, 0)

    for head in range(H):
        part = slice(head * HD, (head + 1) * HD)
        total = sum_ref[head : head + 1, :]
        att_ref[part, :] = att_ref[part, :] / total
        lse_ref[head : head + 1, :] = max_ref[head : head + 1, :] + jnp.log2(total)
    lse_ref[H:, :] = jnp.zeros_like(lse_ref[H:, :])

    def sent(level, carry):
        block = rank - 2 * level
        for group in range(KVH):

            @pl.when(has_up)
            def _():
                z_copy(block, group).wait_send()

            @pl.when((odd == 0) | (level >= 1))
            def _():
                x_copy(block, group).wait_send()

        return carry

    lax.fori_loop(0, depth + 1, sent, 0)


def attend(tokens, seg_row, gain, wq, wk, wv, ranks):
    rows, width = tokens.shape
    vmem = pl.BlockSpec(memory_space=pltpu.VMEM)
    table = jnp.asarray(angle_table(ranks, rows))
    dma = pltpu.SemaphoreType.DMA
    return pl.pallas_call(
        functools.partial(attend_kernel, ranks),
        out_shape=(
            jax.ShapeDtypeStruct((H, PAIR, rows), bf16),
            jax.ShapeDtypeStruct((ranks, KVH, rows + META, PAIR), bf16),
            jax.ShapeDtypeStruct((H * HD, rows), f32),
            jax.ShapeDtypeStruct((16, rows), f32),
        ),
        in_specs=[vmem] * 6 + [pl.BlockSpec(memory_space=pl.ANY)],
        out_specs=(vmem,) * 4,
        scratch_shapes=[
            pltpu.VMEM((HD, rows), f32),
            pltpu.VMEM((16, rows), f32),
            pltpu.VMEM((16, rows), f32),
            dma(()),
            dma((ranks, KVH)),
            dma((ranks, KVH)),
            dma((ranks, KVH)),
        ],
        compiler_params=pltpu.CompilerParams(
            collective_id=0, has_side_effects=True, vmem_limit_bytes=VMEM_LIMIT
        ),
        name="attend",
    )(tokens, seg_row, gain, wq, wk, wv, table)


def mlp_kernel(
    tokens_ref,
    cot_ref,
    att_ref,
    w_out_ref,
    gain_ref,
    w_gate_ref,
    w_up_ref,
    w_down_ref,
    out_ref,
    grads_ref,
    rest_ref,
    gain_grad_ref,
    d_middle_ref,
    dot_ref,
    delta_ref,
):
    rows, width = tokens_ref.shape
    hidden_units = w_gate_ref.shape[1]
    chunk = 512
    inputs = tokens_ref[...].astype(f32)
    attended = att_ref[...].astype(bf16).T
    middle = inputs + dot(attended, w_out_ref[...], 1, 0)
    inverse = lax.rsqrt(jnp.mean(middle * middle, axis=-1, keepdims=True) + epsilon)
    scaled = middle * inverse
    gain = gain_ref[...].astype(f32)
    normed = (scaled * gain).astype(bf16)
    normed_t = normed.T
    cot = cot_ref[...]
    cot_t = cot.T
    result = middle
    d_normed = jnp.zeros((rows, width), f32)

    def put_tiles(first, grad):
        for tile in range(grad.shape[1] // LANES):
            part = grad[:, tile * LANES : (tile + 1) * LANES]
            grads_ref[first // LANES + tile] = part.astype(bf16)

    for first in range(0, hidden_units, chunk):
        part = slice(first, first + chunk)
        gate = dot(normed, w_gate_ref[:, part], 1, 0)
        up = dot(normed, w_up_ref[:, part], 1, 0)
        d_hidden = dot(cot, w_down_ref[part, :], 1, 1)
        sigmoid = jax.nn.sigmoid(gate)
        silu = gate * sigmoid
        hidden = (silu * up).astype(bf16)
        d_gate = (d_hidden * up * (sigmoid + silu * (1.0 - sigmoid))).astype(bf16)
        d_up = (d_hidden * silu).astype(bf16)
        result = result + dot(hidden, w_down_ref[part, :], 1, 0)
        d_normed = d_normed + dot(d_gate, w_gate_ref[:, part], 1, 1)
        d_normed = d_normed + dot(d_up, w_up_ref[:, part], 1, 1)
        put_tiles(first, dot(normed_t, d_gate, 1, 0))
        put_tiles(hidden_units + first, dot(normed_t, d_up, 1, 0))
        put_tiles(2 * hidden_units + first, dot(cot_t, hidden, 1, 0))
    out_ref[...] = result.astype(bf16)
    gain_grad_ref[...] = jnp.sum(d_normed * scaled, axis=0, keepdims=True)
    mixed = d_normed * gain
    d_middle = cot.astype(f32) + inverse * (
        mixed - scaled * jnp.mean(mixed * scaled, axis=-1, keepdims=True)
    )
    d_middle_ref[...] = d_middle
    d_branch = d_middle.astype(bf16)
    whole = width // LANES * LANES
    attended_t = att_ref[...].astype(bf16)
    put_tiles(3 * hidden_units, dot(attended_t, d_branch[:, :whole], 1, 0))
    rest = dot(attended_t, d_branch[:, width - LANES :], 1, 0)
    lane = lax.broadcasted_iota(jnp.int32, rest.shape, 1)
    rest_ref[...] = jnp.where(lane >= LANES - (width - whole), rest, 0.0).astype(bf16)
    d_attended = dot(w_out_ref[...], d_branch, 1, 1).astype(bf16)
    for head in range(H):
        part = slice(head * HD, (head + 1) * HD)
        dot_ref[head, :HD, :] = jnp.zeros((HD, rows), bf16)
        dot_ref[head, HD:, :] = d_attended[part]
        delta_ref[head : head + 1, :] = jnp.sum(
            d_attended[part].astype(f32) * att_ref[part, :], axis=0, keepdims=True
        )
    delta_ref[H:, :] = jnp.zeros_like(delta_ref[H:, :])


def mlp(tokens, cot, att, w_out, gain, w_gate, w_up, w_down):
    rows, width = tokens.shape
    hidden_units = w_gate.shape[1]
    vmem = pl.BlockSpec(memory_space=pltpu.VMEM)
    return pl.pallas_call(
        mlp_kernel,
        out_shape=(
            jax.ShapeDtypeStruct((rows, width), bf16),
            jax.ShapeDtypeStruct(
                ((3 * hidden_units + width) // LANES, width, LANES), bf16
            ),
            jax.ShapeDtypeStruct((width, LANES), bf16),
            jax.ShapeDtypeStruct((1, width), f32),
            jax.ShapeDtypeStruct((rows, width), f32),
            jax.ShapeDtypeStruct((H, PAIR, rows), bf16),
            jax.ShapeDtypeStruct((16, rows), f32),
        ),
        in_specs=[vmem] * 8,
        out_specs=(vmem,) * 7,
        compiler_params=pltpu.CompilerParams(vmem_limit_bytes=VMEM_LIMIT),
        name="mlp",
    )(tokens, cot, att, w_out, gain, w_gate, w_up, w_down)


class Reduction:
    def __init__(self, refs, sems, height, rank, row):
        self.source, self.result, self.half, self.from_core, self.from_xy, self.from_z = refs
        self.send, self.recv = sems
        self.height = height
        self.z, self.x = lax.div(rank, 2), lax.rem(rank, 2)
        self.y, self.core = lax.div(row, 2), lax.rem(row, 2)
        self.core_mate = (rank, row + 1 - 2 * self.core)
        self.y_mate = (rank, row + 2 - 4 * self.y)
        self.x_mate = (rank + 1 - 2 * self.x, row)
        self.row = row
        self.split = TILES // 2
        half, quarter = height // 2, height // 4
        self.first_a, self.first_b = half * self.x, half * self.y
        self.other_a, self.other_b = half - self.first_a, half - self.first_b
        self.quarter_a = self.first_a + quarter * self.y
        self.quarter_b = self.first_b + quarter * self.x
        self.across_a = self.first_a + quarter * (1 - self.y)
        self.across_b = self.first_b + quarter * (1 - self.x)

    def copy(self, src, dst, number, phase, slot, there, target):
        return pltpu.make_async_remote_copy(
            src_ref=src,
            dst_ref=dst,
            send_sem=self.send.at[number, phase, slot],
            recv_sem=self.recv.at[number, phase, there],
            device_id=target,
            device_id_type=MESH,
        )

    def rows(self, first, parts):
        return pl.ds(pl.multiple_of(first, 16), self.height // parts)

    def tiles(self, number, core):
        return pl.ds(number * 2 * TILES + core * TILES, TILES)

    def quarter_of(self, tile):
        return jnp.where(tile < self.split, self.quarter_a, self.quarter_b)

    def copies(self, number, phase):
        head, tail = pl.ds(0, self.split), pl.ds(self.split, TILES - self.split)
        base = number * 2 * TILES + self.core * TILES
        out_head = pl.ds(base, self.split)
        out_tail = pl.ds(base + self.split, TILES - self.split)
        if phase == 0:
            src = self.source.at[self.tiles(number, 1 - self.core)]
            dst = self.from_core.at[number]
            return [self.copy(src, dst, number, 0, 0, 0, self.core_mate)]
        if phase in (1, 2):
            parts = 2 * phase
            row_a = self.rows(self.other_a if phase == 1 else self.across_a, parts)
            row_b = self.rows(self.other_b if phase == 1 else self.across_b, parts)
            size = self.height // parts
            first = 0 if phase == 1 else self.height // 2
            mates = (self.x_mate, self.y_mate) if phase == 1 else (self.y_mate, self.x_mate)
            return [
                self.copy(
                    self.half.at[number, part, row],
                    self.from_xy.at[number, part, pl.ds(first, size)],
                    number,
                    phase,
                    slot,
                    slot,
                    mates[slot],
                )
                for slot, (part, row) in enumerate(((head, row_a), (tail, row_b)))
            ]
        if phase in (3, 4):
            made = []
            for step in range(1, TILES):
                other = lax.rem(self.z + step, TILES)
                target = (2 * other + self.x, self.row)
                if phase == 3:
                    src = self.half.at[number, other, self.rows(self.quarter_of(other), 4)]
                    dst = self.from_z.at[number, self.z]
                else:
                    src = self.result.at[base + self.z, self.rows(self.quarter_of(self.z), 4)]
                    dst = src
                made.append(self.copy(src, dst, number, phase, other, self.z, target))
            return made
        if phase in (5, 6):
            parts = 4 if phase == 5 else 2
            row_a = self.rows(self.quarter_a if phase == 5 else self.first_a, parts)
            row_b = self.rows(self.quarter_b if phase == 5 else self.first_b, parts)
            mates = (self.y_mate, self.x_mate) if phase == 5 else (self.x_mate, self.y_mate)
            return [
                self.copy(
                    self.result.at[part, row],
                    self.result.at[part, row],
                    number,
                    phase,
                    slot,
                    slot,
                    mates[slot],
                )
                for slot, (part, row) in enumerate(((out_head, row_a), (out_tail, row_b)))
            ]
        place = self.result.at[self.tiles(number, self.core)]
        return [self.copy(place, place, number, 7, 0, 0, self.core_mate)]

    def arrivals(self, number, phase):
        if phase not in (3, 4):
            return self.copies(number, phase)
        made = []
        base = number * 2 * TILES + self.core * TILES
        for step in range(1, TILES):
            other = lax.rem(self.z + step, TILES)
            target = (2 * other + self.x, self.row)
            if phase == 3:
                dst = self.from_z.at[number, other]
            else:
                dst = self.result.at[base + other, self.rows(self.quarter_of(other), 4)]
            made.append(self.copy(dst, dst, number, phase, other, other, target))
        return made

    def start(self, number, phase):
        for made in self.copies(number, phase):
            made.start()

    def finish(self, number, phase):
        for made in self.arrivals(number, phase):
            made.wait_recv()
        head, tail = pl.ds(0, self.split), pl.ds(self.split, TILES - self.split)
        if phase == 0:
            own = self.source[self.tiles(number, self.core)].astype(f32)
            self.half[number] = (own + self.from_core[number].astype(f32)).astype(bf16)
        if phase in (1, 2):
            parts = 2 * phase
            size = self.height // parts
            first = 0 if phase == 1 else self.height // 2
            row_a = self.rows(self.first_a if phase == 1 else self.quarter_a, parts)
            row_b = self.rows(self.first_b if phase == 1 else self.quarter_b, parts)
            for part, row in ((head, row_a), (tail, row_b)):
                other = self.from_xy[number, part, first : first + size].astype(f32)
                own = self.half[number, part, row].astype(f32)
                self.half[number, part, row] = (own + other).astype(bf16)
        if phase == 3:
            row = self.rows(self.quarter_of(self.z), 4)
            total = self.half[number, self.z, row].astype(f32)
            for step in range(1, TILES):
                other = lax.rem(self.z + step, TILES)
                total = total + self.from_z[number, other].astype(f32)
            base = number * 2 * TILES + self.core * TILES
            self.result[base + self.z, row] = total.astype(bf16)

    def event(self, number, phase):
        if phase > 0:
            self.finish(number, phase - 1)
        if phase < 8:
            self.start(number, phase)

    def drain(self, number):
        for phase in range(8):
            for made in self.copies(number, phase):
                made.wait_send()


def reduction_scratch(numbers, height):
    dma = pltpu.SemaphoreType.DMA
    return [
        pltpu.VMEM((numbers, TILES, height, LANES), bf16),
        pltpu.VMEM((numbers, TILES, height, LANES), bf16),
        pltpu.VMEM((numbers, TILES, height * 3 // 4, LANES), bf16),
        pltpu.VMEM((numbers, TILES, height // 4, LANES), bf16),
        dma((numbers, 8, TILES)),
        dma((numbers, 8, TILES)),
    ]


def back_kernel(
    ranks,
    reduce_here,
    tokens_ref,
    seg_ref,
    gain_ref,
    wq_ref,
    wk_ref,
    wv_ref,
    table_ref,
    qt_ref,
    kv_ref,
    lse_ref,
    dot_ref,
    delta_ref,
    d_middle_ref,
    source_ref,
    rest_ref,
    gain_mlp_ref,
    out_ref,
    grads_ref,
    late_ref,
    turn_ref,
    bias_ref,
    acc_ref,
    d_all_ref,
    terms_ref,
    off_out_ref,
    off_in_ref,
    z_out_ref,
    z_in_ref,
    turn_sem,
    off_send,
    off_recv,
    z_send,
    z_recv,
    *reduction_refs,
):
    rank = lax.axis_index("seq")
    row = lax.axis_index("batch")
    rows, width = tokens_ref.shape
    levels = ranks // 2
    depth = lax.div(rank, 2)
    odd = lax.rem(rank, 2)
    mate = rank + 1 - 2 * odd

    turn_copy = pltpu.make_async_copy(table_ref.at[rank], turn_ref, turn_sem)
    turn_copy.start()
    barrier = pltpu.get_barrier_semaphore()
    peers = [(mate, row)]
    for step in range(1, levels):
        peers.append((2 * lax.rem(depth + step, levels) + odd, row))
    if reduce_here:
        core = lax.rem(row, 2)
        peers.append((rank, row + 1 - 2 * core))
        peers.append((rank, row + 2 - 4 * lax.div(row, 2)))
    for peer in peers:
        pl.semaphore_signal(barrier, inc=1, device_id=peer, device_id_type=MESH)
    pl.semaphore_wait(barrier, len(peers))

    schedule = {}
    after_loop = []
    rounds = 0
    if reduce_here:
        early_scratch, late_scratch = reduction_refs[:6], reduction_refs[6:12]
        late_source = reduction_refs[12]
        rounds = source_ref.shape[0] // (2 * TILES)
        early = Reduction(
            (source_ref, grads_ref) + early_scratch[:4], early_scratch[4:], width, rank, row
        )
        last = Reduction(
            (late_source, late_ref) + late_scratch[:4],
            late_scratch[4:],
            width + EXTRA,
            rank,
            row,
        )
        for number in range(rounds):
            early.start(number, 0)
        for diagonal in range(1, rounds + 8):
            events = [
                (number, diagonal - number)
                for number in range(rounds)
                if 1 <= diagonal - number <= 8
            ]
            place = 1 + SPACING * (diagonal - 1)
            if place < KVH * ranks:
                schedule[place] = events
            else:
                after_loop.append(events)
    else:
        late_source = late_ref

    seg_row = seg_ref[...]
    in_long = long_row(seg_row)
    acc_ref[...] = jnp.zeros_like(acc_ref)

    def off_copy(slot, group):
        return pltpu.make_async_remote_copy(
            src_ref=off_out_ref.at[slot, group],
            dst_ref=off_in_ref.at[slot, group],
            send_sem=off_send.at[slot, group],
            recv_sem=off_recv.at[slot, group],
            device_id=(mate, row),
            device_id_type=MESH,
        )

    def z_copy(slot, group):
        return pltpu.make_async_remote_copy(
            src_ref=z_out_ref.at[slot, group],
            dst_ref=z_in_ref.at[slot, group],
            send_sem=z_send.at[slot, group],
            recv_sem=z_recv.at[slot, group],
            device_id=(rank - 2, row),
            device_id_type=MESH,
        )

    def pair_step(block, group, masked):
        pair = kv_ref[block, group, :rows, :]
        keys_t = pair.T[:HD]
        heads = range(group * GROUP, (group + 1) * GROUP)
        old = [acc_ref[head] for head in heads]
        total = jnp.zeros((rows, PAIR), f32)
        results = []
        for spot, head in enumerate(heads):
            scores = dot(pair, qt_ref[head], 1, 0)
            level = lse_ref[head : head + 1, :]
            if masked:
                scores = scores + bias_ref[...]
            else:
                level = jnp.where(in_long, level, never)
            probs = jnp.exp2(scores - level)
            d_probs = dot(pair, dot_ref[head], 1, 0)
            d_scores = (probs * (d_probs - delta_ref[head : head + 1, :])).astype(bf16)
            total = total + dot(probs.astype(bf16), dot_ref[head], 1, 1)
            total = total + dot(d_scores, qt_ref[head], 1, 1)
            results.append(old[spot] + dot(keys_t, d_scores, 1, 0))
        for spot, head in enumerate(heads):
            acc_ref[head] = results[spot]
        slot = lax.div(block, 2)
        straight = lax.rem(block, 2) == odd
        low = total.astype(bf16)

        @pl.when(straight)
        def _():
            terms_ref[slot, group] = low

        @pl.when(jnp.logical_not(straight))
        def _():
            off_out_ref[slot, group] = low
            off_copy(slot, group).start()

    def combine(time):
        block = time - (levels - depth)
        valid = (block >= 0) & (block <= rank) & (lax.rem(block + 2 * levels, 2) == odd)
        slot = lax.div(jnp.maximum(block, 0), 2)
        from_mate = valid & (mate > block)
        from_above = valid & (depth < levels - 1)
        owner = valid & (block == rank)
        for group in range(KVH):

            @pl.when(from_mate)
            def _():
                off_copy(slot, group).wait_recv()

            @pl.when(from_above)
            def _():
                z_copy(slot, group).wait_recv()

            @pl.when(valid)
            def _():
                total = terms_ref[slot, group].astype(f32)
                total = total + jnp.where(from_mate, off_in_ref[slot, group].astype(f32), 0.0)
                total = total + jnp.where(from_above, z_in_ref[slot, group].astype(f32), 0.0)
                z_out_ref[slot, group] = total.astype(bf16)

            @pl.when(valid & jnp.logical_not(owner))
            def _():
                z_copy(slot, group).start()

    def step(block, carry):
        @pl.when((block == 0) & (rank > 0))
        def _():
            key_bias = first_bias(kv_ref[0, 0, rows:, :], rows)
            bias_ref[...] = key_bias + jnp.where(in_long, 0.0, masked_value)

        @pl.when(block == rank)
        def _():
            bias_ref[...] = own_bias(seg_row)

        masked = (block == 0) | (block == rank)
        for group in range(KVH):

            @pl.when(masked)
            def _():
                pair_step(block, group, True)

            @pl.when(jnp.logical_not(masked) & (block < rank))
            def _():
                pair_step(block, group, False)

            for place, events in schedule.items():
                if place % KVH == group:

                    @pl.when(block == place // KVH)
                    def _():
                        for number, phase in events:
                            early.event(number, phase)

        combine(block)
        return carry

    lax.fori_loop(0, ranks, step, 0)
    combine(ranks)

    turn_copy.wait()
    cosine = turn_ref[: HD // 2]
    sine = turn_ref[HD // 2 :]
    q_cols, k_cols = H * HD, KVH * HD
    for head in range(H):
        turned = turn_back(acc_ref[head] * HD**-0.5, cosine, sine)
        d_all_ref[head * HD : (head + 1) * HD, :] = turned.astype(bf16)
    for group in range(KVH):
        both = z_out_ref[depth, group].astype(f32).T
        first = q_cols + group * HD
        turned = turn_back(both[:HD] * LN2, cosine, sine)
        d_all_ref[first : first + HD, :] = turned.astype(bf16)
        d_all_ref[first + k_cols : first + k_cols + HD, :] = both[HD:].astype(bf16)
    used = q_cols + 2 * k_cols
    d_all_ref[used:, :] = jnp.zeros((d_all_ref.shape[0] - used, rows), bf16)
    inputs = tokens_ref[...].astype(f32)
    inverse = lax.rsqrt(jnp.mean(inputs * inputs, axis=-1, keepdims=True) + epsilon)
    scaled = inputs * inverse
    gain = gain_ref[...].astype(f32)
    normed_t = (scaled * gain).astype(bf16).T
    d_normed = (
        dot(d_all_ref[:q_cols], wq_ref[...], 0, 1)
        + dot(d_all_ref[q_cols : q_cols + k_cols], wk_ref[...], 0, 1)
        + dot(d_all_ref[q_cols + k_cols : used], wv_ref[...], 0, 1)
    )
    gain_attn = jnp.sum(d_normed * scaled, axis=0, keepdims=True)
    spot = lax.broadcasted_iota(jnp.int32, (EXTRA, LANES), 0)
    for tile in range(2 * TILES):
        part = slice(tile * LANES, (tile + 1) * LANES)
        grad = dot(normed_t, d_all_ref[part], 1, 1)
        if tile == 2 * TILES - 1:
            grad = grad + rest_ref[...].astype(f32)
        late_source[tile, :width, :] = grad.astype(bf16)
        left = min(width - tile * LANES, LANES)
        if left > 0:
            chosen = slice(tile * LANES, tile * LANES + left)
            pad = jnp.zeros((1, LANES - left), f32)
            first, second = gain_attn[:, chosen], gain_mlp_ref[:, chosen]
            if left < LANES:
                first = jnp.concatenate([first, pad], axis=1)
                second = jnp.concatenate([second, pad], axis=1)
            extra = jnp.where(spot == 0, first, jnp.where(spot == 1, second, 0.0))
        else:
            extra = jnp.zeros((EXTRA, LANES), f32)
        late_source[tile, width:, :] = extra.astype(bf16)

    if reduce_here:
        last.start(0, 0)
    mixed = d_normed * gain
    out_ref[...] = d_middle_ref[...] + inverse * (
        mixed - scaled * jnp.mean(mixed * scaled, axis=-1, keepdims=True)
    )
    if reduce_here:
        for phase in range(1, 9):
            if after_loop:
                for number, early_phase in after_loop.pop(0):
                    early.event(number, early_phase)
            last.event(0, phase)
        for events in after_loop:
            for number, early_phase in events:
                early.event(number, early_phase)
        for number in range(rounds):
            early.drain(number)
        last.drain(0)
    else:
        grads_ref[...] = source_ref[...]

    def sent(block, carry):
        slot = lax.div(block, 2)
        straight = lax.rem(block, 2) == odd
        for group in range(KVH):

            @pl.when(jnp.logical_not(straight))
            def _():
                off_copy(slot, group).wait_send()

            @pl.when(straight & (block < rank))
            def _():
                z_copy(slot, group).wait_send()

        return carry

    lax.fori_loop(0, rank + 1, sent, 0)


def back(
    ranks,
    reduce_here,
    tokens,
    seg_row,
    gain,
    wq,
    wk,
    wv,
    qt,
    kv,
    lse,
    dot_t,
    delta,
    d_middle,
    grads,
    rest,
    gain_mlp,
):
    rows, width = tokens.shape
    levels = ranks // 2
    vmem = pl.BlockSpec(memory_space=pltpu.VMEM)
    table = jnp.asarray(angle_table(ranks, rows))
    dma = pltpu.SemaphoreType.DMA
    late_shape = (2 * TILES, width + EXTRA, LANES)
    scratch = [
        pltpu.VMEM((HD, rows), f32),
        pltpu.VMEM((rows, rows), f32),
        pltpu.VMEM((H, HD, rows), f32),
        pltpu.VMEM((2 * TILES * LANES, rows), bf16),
    ]
    scratch += [pltpu.VMEM((levels, KVH, rows, PAIR), bf16)] * 5
    scratch += [dma(())] + [dma((levels, KVH))] * 4
    if reduce_here:
        scratch += reduction_scratch(grads.shape[0] // (2 * TILES), width)
        scratch += reduction_scratch(1, width + EXTRA)
        scratch += [pltpu.VMEM(late_shape, bf16)]
    return pl.pallas_call(
        functools.partial(back_kernel, ranks, reduce_here),
        out_shape=(
            jax.ShapeDtypeStruct((rows, width), f32),
            jax.ShapeDtypeStruct(grads.shape, bf16),
            jax.ShapeDtypeStruct(late_shape, bf16),
        ),
        in_specs=[vmem] * 6 + [pl.BlockSpec(memory_space=pl.ANY)] + [vmem] * 9,
        out_specs=(vmem,) * 3,
        scratch_shapes=scratch,
        compiler_params=pltpu.CompilerParams(
            collective_id=1, has_side_effects=True, vmem_limit_bytes=VMEM_LIMIT
        ),
        name="back",
    )(
        tokens,
        seg_row,
        gain,
        wq,
        wk,
        wv,
        table,
        qt,
        kv,
        lse,
        dot_t,
        delta,
        d_middle,
        grads,
        rest,
        gain_mlp,
    )


def finish_kernel(
    gate_ref,
    up_ref,
    down_ref,
    grads_ref,
    late_ref,
    gain_attn_ref,
    query_ref,
    key_ref,
    value_ref,
    out_ref,
    gain_mlp_ref,
    grad_gate_ref,
    grad_up_ref,
    grad_down_ref,
):
    width = query_ref.shape[0]
    grad_gate_ref[...] = gate_ref[0].astype(f32)
    grad_up_ref[...] = up_ref[0].astype(f32)
    grad_down_ref[...] = down_ref[0].astype(f32).T

    @pl.when(pl.program_id(0) == 0)
    def _():
        late = jnp.concatenate(
            [late_ref[tile, :width, :].astype(f32) for tile in range(2 * TILES)], axis=1
        )
        q_cols, k_cols = H * HD, KVH * HD
        used = q_cols + 2 * k_cols
        query_ref[...] = late[:, :q_cols]
        key_ref[...] = late[:, q_cols : q_cols + k_cols]
        value_ref[...] = late[:, q_cols + k_cols : used]
        whole = grads_ref.shape[0]
        for tile in range(whole):
            out_ref[:, tile * LANES : (tile + 1) * LANES] = grads_ref[tile].astype(f32)
        out_ref[:, whole * LANES :] = late[:, used : used + width - whole * LANES]
        for tile in range(-(-width // LANES)):
            left = min(width - tile * LANES, LANES)
            chosen = slice(tile * LANES, tile * LANES + left)
            gain_attn_ref[:, chosen] = late_ref[tile, width : width + 16, :left].astype(f32)[0:1]
            gain_mlp_ref[:, chosen] = late_ref[tile, width : width + 16, :left].astype(f32)[1:2]


def finish(grads, late, width, hidden_units):
    vmem = pl.BlockSpec(memory_space=pltpu.VMEM)
    tiles = hidden_units // LANES
    whole = width // LANES
    fixed = lambda shape: pl.BlockSpec(shape, lambda i: (0,) * len(shape))
    tile_at = lambda base: pl.BlockSpec((1, width, LANES), lambda i: (base + i, 0, 0))
    k_cols = KVH * HD
    return pl.pallas_call(
        finish_kernel,
        grid=(tiles,),
        out_shape=(
            jax.ShapeDtypeStruct((1, width), f32),
            jax.ShapeDtypeStruct((width, H * HD), f32),
            jax.ShapeDtypeStruct((width, k_cols), f32),
            jax.ShapeDtypeStruct((width, k_cols), f32),
            jax.ShapeDtypeStruct((H * HD, width), f32),
            jax.ShapeDtypeStruct((1, width), f32),
            jax.ShapeDtypeStruct((width, hidden_units), f32),
            jax.ShapeDtypeStruct((width, hidden_units), f32),
            jax.ShapeDtypeStruct((hidden_units, width), f32),
        ),
        in_specs=[
            tile_at(0),
            tile_at(tiles),
            tile_at(2 * tiles),
            pl.BlockSpec((whole, width, LANES), lambda i: (3 * tiles // whole, 0, 0)),
            fixed(late.shape),
        ],
        out_specs=(
            fixed((1, width)),
            fixed((width, H * HD)),
            fixed((width, k_cols)),
            fixed((width, k_cols)),
            fixed((H * HD, width)),
            fixed((1, width)),
            pl.BlockSpec((width, LANES), lambda i: (0, i)),
            pl.BlockSpec((width, LANES), lambda i: (0, i)),
            pl.BlockSpec((LANES, width), lambda i: (i, 0)),
        ),
        compiler_params=pltpu.CompilerParams(vmem_limit_bytes=VMEM_LIMIT),
        name="finish",
    )(grads, grads, grads, grads, late)


def local(
    ranks,
    batches,
    tokens,
    segment_ids,
    gain_attn,
    w_query,
    w_key,
    w_value,
    w_out,
    gain_mlp,
    w_gate,
    w_up,
    w_down,
    cotangent,
):
    rows, width = tokens.shape[1:]
    both_axes = ("seq", "batch")
    gain_first = gain_attn.reshape(1, width)
    gain_second = gain_mlp.reshape(1, width)
    qt, kv, att, lse = attend(
        tokens[0], segment_ids, gain_first, w_query, w_key, w_value, ranks
    )
    output, grads, rest, grad_gain_mlp, d_middle, dot_t, delta = mlp(
        tokens[0], cotangent[0], att, w_out, gain_second, w_gate, w_up, w_down
    )
    reduce_here = ranks == 2 * TILES and batches == 4
    d_inputs, reduced, late = back(
        ranks,
        reduce_here,
        tokens[0],
        segment_ids,
        gain_first,
        w_query,
        w_key,
        w_value,
        qt,
        kv,
        lse,
        dot_t,
        delta,
        d_middle,
        grads if reduce_here else rest[None],
        rest,
        grad_gain_mlp,
    )
    if not reduce_here:
        reduced, late = lax.psum((grads, late), both_axes)
    (
        grad_gain_attn,
        grad_query,
        grad_key,
        grad_value,
        grad_out,
        grad_gain_mlp,
        grad_gate,
        grad_up,
        grad_down,
    ) = finish(reduced, late, width, w_gate.shape[1])
    return (
        output[None],
        d_inputs[None],
        grad_gain_attn[0],
        grad_query,
        grad_key,
        grad_value,
        grad_out,
        grad_gain_mlp[0],
        grad_gate,
        grad_up,
        grad_down,
    )


def solution(mesh):
    split = P("batch", "seq", None)
    return jax.shard_map(
        functools.partial(local, mesh.shape["seq"], mesh.shape["batch"]),
        mesh=mesh,
        in_specs=(split, P("batch", "seq")) + (P(),) * 9 + (split,),
        out_specs=(split, split) + (P(),) * 9,
        check_vma=False,
    )
```

```python
import functools

import jax
import jax.numpy as jnp
import numpy as np
from jax import lax
from jax.experimental import pallas as pl
from jax.experimental.pallas import tpu as pltpu
from jax.sharding import PartitionSpec as P

H = 9
KVH = 3
HD = 64
GROUP = H // KVH
PAIR = 2 * HD
META = 16
LANES = 128
TILES = 4
EXTRA = 64
SPACING = 2
FINISH_STEPS = 4

epsilon = 1e-05
theta_base = 10000.0
masked_value = -1e30
never = 1e30
LOG2E = 1.4426950408889634
LN2 = 0.6931471805599453
MESH = pl.DeviceIdType.MESH
f32 = jnp.float32
bf16 = jnp.bfloat16
VMEM_LIMIT = 60 * 2**20


def dot(left, right, left_dim, right_dim):
    return lax.dot_general(
        left,
        right,
        (((left_dim,), (right_dim,)), ((), ())),
        preferred_element_type=f32,
    )


def angle_table(ranks, rows):
    half = HD // 2
    freqs = theta_base ** (-2.0 * np.arange(half, dtype=np.float64) / HD)
    angles = freqs[:, None] * np.arange(ranks * rows, dtype=np.float64)[None, :]
    table = np.concatenate([np.cos(angles), np.sin(angles)], axis=0).astype(np.float32)
    return np.ascontiguousarray(table.reshape(HD, ranks, rows).transpose(1, 0, 2))


def turn(vectors, cosine, sine):
    half = HD // 2
    first, second = vectors[:half], vectors[half:]
    return jnp.concatenate(
        [first * cosine - second * sine, second * cosine + first * sine], axis=0
    )


def column(vector, rows):
    wide = jnp.broadcast_to(vector.astype(f32).reshape(1, rows), (128, rows))
    return wide.T[:, :1]


def norm_parts(inputs):
    mean = jnp.mean(inputs * inputs, axis=0, keepdims=True)
    inverse = lax.rsqrt(mean + epsilon)
    return inverse, inputs * inverse


def turn_back(vectors, cosine, sine):
    half = HD // 2
    first, second = vectors[:half], vectors[half:]
    return jnp.concatenate(
        [first * cosine + second * sine, second * cosine - first * sine], axis=0
    )


def own_bias(seg_row):
    rows = seg_row.shape[1]
    ids = seg_row.astype(f32)
    columns = jnp.broadcast_to(ids, (128, rows)).T[:, :1]
    key = lax.broadcasted_iota(jnp.int32, (rows, rows), 0)
    query = lax.broadcasted_iota(jnp.int32, (rows, rows), 1)
    visible = (columns == ids) & (key <= query)
    return jnp.where(visible, 0.0, masked_value)


def long_row(seg_row):
    return seg_row == seg_row[:, :1]


def first_bias(meta, rows):
    start = 2.0 * meta[0:1, :1].astype(f32) + meta[1:2, :1].astype(f32)
    key = lax.broadcasted_iota(jnp.int32, (rows, 1), 0).astype(f32)
    return jnp.where(key >= start, 0.0, masked_value)


def attend_kernel(
    ranks,
    tokens_ref,
    seg_ref,
    gain_ref,
    wq_ref,
    wk_ref,
    wv_ref,
    table_ref,
    qt_ref,
    kv_ref,
    att_ref,
    lse_ref,
    turn_ref,
    max_ref,
    sum_ref,
    turn_sem,
    z_sem,
    x_sem,
    in_sem,
):
    rank = lax.axis_index("seq")
    row = lax.axis_index("batch")
    width, rows = tokens_ref.shape
    depth = lax.div(rank, 2)
    odd = lax.rem(rank, 2)
    mate = rank + 1 - 2 * odd
    has_up = rank + 2 < ranks
    has_down = rank >= 2

    turn_copy = pltpu.make_async_copy(table_ref.at[rank], turn_ref, turn_sem)
    turn_copy.start()

    barrier = pltpu.get_barrier_semaphore()
    pl.semaphore_signal(barrier, inc=1, device_id=(mate, row), device_id_type=MESH)

    @pl.when(has_up)
    def _():
        pl.semaphore_signal(barrier, inc=1, device_id=(rank + 2, row), device_id_type=MESH)

    @pl.when(has_down)
    def _():
        pl.semaphore_signal(barrier, inc=1, device_id=(rank - 2, row), device_id_type=MESH)

    def z_copy(block, group):
        return pltpu.make_async_remote_copy(
            src_ref=kv_ref.at[block, group],
            dst_ref=kv_ref.at[block, group],
            send_sem=z_sem.at[block, group],
            recv_sem=in_sem.at[block, group],
            device_id=(rank + 2, row),
            device_id_type=MESH,
        )

    def x_copy(block, group):
        return pltpu.make_async_remote_copy(
            src_ref=kv_ref.at[block, group],
            dst_ref=kv_ref.at[block, group],
            send_sem=x_sem.at[block, group],
            recv_sem=in_sem.at[block, group],
            device_id=(mate, row),
            device_id_type=MESH,
        )

    unused, scaled = norm_parts(tokens_ref[...].astype(f32))
    normed = (scaled * column(gain_ref[...], width)).astype(bf16)
    keys = dot(wk_ref[...], normed, 1, 0)
    values = dot(wv_ref[...], normed, 1, 0)
    seg_row = seg_ref[...]
    start = jnp.sum((seg_row != seg_row[:, rows - 1 :]).astype(f32), axis=1, keepdims=True)
    high = jnp.floor(0.5 * start)
    low = start - 2.0 * high
    which = lax.broadcasted_iota(jnp.int32, (META, PAIR), 0)
    meta = jnp.where(which == 0, high, jnp.where(which == 1, low, 0.0)).astype(bf16)
    turn_copy.wait()
    cosine = turn_ref[: HD // 2]
    sine = turn_ref[HD // 2 :]
    for group in range(KVH):
        part = slice(group * HD, group * HD + HD)
        both = jnp.concatenate([turn(keys[part], cosine, sine), values[part]], axis=0)
        kv_ref[rank, group, :rows, :] = both.astype(bf16).T
        kv_ref[rank, group, rows:, :] = meta

    pl.semaphore_wait(barrier, 1 + has_up.astype(jnp.int32) + has_down.astype(jnp.int32))
    for group in range(KVH):

        @pl.when(odd == 0)
        def _():
            x_copy(rank, group).start()

        @pl.when(has_up)
        def _():
            z_copy(rank, group).start()

    def relay(level, group):
        block = rank - 2 * level
        z_in = pltpu.make_async_remote_copy(
            src_ref=kv_ref.at[block, group],
            dst_ref=kv_ref.at[block, group],
            send_sem=z_sem.at[block, group],
            recv_sem=in_sem.at[block, group],
            device_id=(mate, row),
            device_id_type=MESH,
        )
        z_in.wait_recv()
        x_copy(block, group).start()

        @pl.when(has_up)
        def _():
            z_copy(block, group).start()

    queries = dot(wq_ref[...], normed, 0, 0)
    for head in range(H):
        part = slice(head * HD, head * HD + HD)
        turned = turn(queries[part], cosine, sine) * (LOG2E / HD**0.5)
        qt_ref[head, :HD, :] = turned.astype(bf16)
        qt_ref[head, HD:, :] = jnp.zeros((HD, rows), bf16)

    bias = own_bias(seg_row)
    for group in range(KVH):
        pair = kv_ref[rank, group, :rows, :]
        values_t = pair.T[HD:]
        for head in range(group * GROUP, (group + 1) * GROUP):
            scores = dot(pair, qt_ref[head], 1, 0) + bias
            top = jnp.max(scores, axis=0, keepdims=True)
            weights = jnp.exp2(scores - top)
            max_ref[head : head + 1, :] = top
            sum_ref[head : head + 1, :] = jnp.sum(weights, axis=0, keepdims=True)
            att_ref[head * HD : (head + 1) * HD, :] = dot(values_t, weights.astype(bf16), 1, 0)

        @pl.when(depth >= 1)
        def _():
            relay(1, group)

    in_long = long_row(seg_row)

    def block_step(block, group, key_bias):
        pair = kv_ref[block, group, :rows, :]
        values_t = pair.T[HD:]
        heads = range(group * GROUP, (group + 1) * GROUP)
        old_max = [max_ref[head : head + 1, :] for head in heads]
        old_sum = [sum_ref[head : head + 1, :] for head in heads]
        old_att = [att_ref[head * HD : (head + 1) * HD, :] for head in heads]
        results = []
        for spot, head in enumerate(heads):
            scores = dot(pair, qt_ref[head], 1, 0)
            if key_bias is not None:
                scores = scores + key_bias
            top = jnp.maximum(old_max[spot], jnp.max(scores, axis=0, keepdims=True))
            top = jnp.where(in_long, top, old_max[spot])
            weights = jnp.exp2(scores - jnp.where(in_long, top, never))
            scale = jnp.exp2(old_max[spot] - top)
            results.append(
                (
                    top,
                    old_sum[spot] * scale + jnp.sum(weights, axis=0, keepdims=True),
                    old_att[spot] * scale + dot(values_t, weights.astype(bf16), 1, 0),
                )
            )
        for spot, head in enumerate(heads):
            max_ref[head : head + 1, :] = results[spot][0]
            sum_ref[head : head + 1, :] = results[spot][1]
            att_ref[head * HD : (head + 1) * HD, :] = results[spot][2]

    def step(index, carry):
        level = lax.div(index + 1, 2)
        straight = lax.rem(index, 2) == 1
        block = jnp.where(straight, rank, mate) - 2 * level
        for group in range(KVH):

            @pl.when(straight & (level + 1 <= depth))
            def _():
                relay(level + 1, group)

            @pl.when(jnp.logical_not(straight))
            def _():
                x_copy(block, group).wait_recv()

            @pl.when(block == 0)
            def _():
                key_bias = first_bias(kv_ref[0, group, rows:, :], rows)
                block_step(block, group, key_bias)

            @pl.when(block != 0)
            def _():
                block_step(block, group, None)

        return carry

    lax.fori_loop(1 - odd, 2 * depth + 1, step, 0)

    for head in range(H):
        part = slice(head * HD, (head + 1) * HD)
        total = sum_ref[head : head + 1, :]
        att_ref[part, :] = att_ref[part, :] / total
        lse_ref[head : head + 1, :] = max_ref[head : head + 1, :] + jnp.log2(total)
    lse_ref[H:, :] = jnp.zeros_like(lse_ref[H:, :])

    def sent(level, carry):
        block = rank - 2 * level
        for group in range(KVH):

            @pl.when(has_up)
            def _():
                z_copy(block, group).wait_send()

            @pl.when((odd == 0) | (level >= 1))
            def _():
                x_copy(block, group).wait_send()

        return carry

    lax.fori_loop(0, depth + 1, sent, 0)


def attend(tokens, seg_row, gain, wq, wk, wv, ranks):
    width, rows = tokens.shape
    vmem = pl.BlockSpec(memory_space=pltpu.VMEM)
    table = jnp.asarray(angle_table(ranks, rows))
    dma = pltpu.SemaphoreType.DMA
    return pl.pallas_call(
        functools.partial(attend_kernel, ranks),
        out_shape=(
            jax.ShapeDtypeStruct((H, PAIR, rows), bf16),
            jax.ShapeDtypeStruct((ranks, KVH, rows + META, PAIR), bf16),
            jax.ShapeDtypeStruct((H * HD, rows), f32),
            jax.ShapeDtypeStruct((16, rows), f32),
        ),
        in_specs=[vmem] * 6 + [pl.BlockSpec(memory_space=pl.ANY)],
        out_specs=(vmem,) * 4,
        scratch_shapes=[
            pltpu.VMEM((HD, rows), f32),
            pltpu.VMEM((16, rows), f32),
            pltpu.VMEM((16, rows), f32),
            dma(()),
            dma((ranks, KVH)),
            dma((ranks, KVH)),
            dma((ranks, KVH)),
        ],
        compiler_params=pltpu.CompilerParams(
            collective_id=0, has_side_effects=True, vmem_limit_bytes=VMEM_LIMIT
        ),
        name="attend",
    )(tokens, seg_row, gain, wq, wk, wv, table)


def mlp_kernel(
    tokens_ref,
    cot_ref,
    att_ref,
    w_out_ref,
    gain_ref,
    w_gate_ref,
    w_up_ref,
    w_down_ref,
    out_ref,
    grads_ref,
    rest_ref,
    gain_grad_ref,
    d_middle_ref,
    dot_ref,
    delta_ref,
):
    width, rows = tokens_ref.shape
    hidden_units = w_gate_ref.shape[1]
    chunk = 512
    attended = att_ref[...].astype(bf16)
    middle = tokens_ref[...].astype(f32) + dot(w_out_ref[...], attended, 0, 0)
    inverse, scaled = norm_parts(middle)
    gain = column(gain_ref[...], width)
    normed_t = (scaled * gain).astype(bf16)
    normed = normed_t.T
    cot_t = cot_ref[...]
    cot = cot_t.T
    result = middle
    d_normed = jnp.zeros((width, rows), f32)

    def put_tiles(first, grad):
        for tile in range(grad.shape[1] // LANES):
            part = grad[:, tile * LANES : (tile + 1) * LANES]
            grads_ref[first // LANES + tile] = part.astype(bf16)

    for first in range(0, hidden_units, chunk):
        part = slice(first, first + chunk)
        gate = dot(normed, w_gate_ref[:, part], 1, 0)
        up = dot(normed, w_up_ref[:, part], 1, 0)
        d_hidden = dot(cot, w_down_ref[:, part], 1, 0)
        sigmoid = jax.nn.sigmoid(gate)
        silu = gate * sigmoid
        hidden = (silu * up).astype(bf16)
        d_gate = (d_hidden * up * (sigmoid + silu * (1.0 - sigmoid))).astype(bf16)
        d_up = (d_hidden * silu).astype(bf16)
        result = result + dot(w_down_ref[:, part], hidden, 1, 1)
        d_normed = d_normed + dot(w_gate_ref[:, part], d_gate, 1, 1)
        d_normed = d_normed + dot(w_up_ref[:, part], d_up, 1, 1)
        put_tiles(first, dot(normed_t, d_gate, 1, 0))
        put_tiles(hidden_units + first, dot(normed_t, d_up, 1, 0))
        put_tiles(2 * hidden_units + first, dot(cot_t, hidden, 1, 0))
    out_ref[...] = result.astype(bf16)
    gain_grad = jnp.sum(d_normed * scaled, axis=1, keepdims=True)
    gain_grad_ref[...] = jnp.broadcast_to(gain_grad, (width, LANES)).T[:1]
    mixed = d_normed * gain
    d_middle = cot_t.astype(f32) + inverse * (
        mixed - scaled * jnp.mean(mixed * scaled, axis=0, keepdims=True)
    )
    d_middle_ref[...] = d_middle
    d_branch = d_middle.astype(bf16)
    whole = width // LANES * LANES
    put_tiles(3 * hidden_units, dot(attended, d_branch[:whole], 1, 1))
    rest = dot(attended, d_branch[width - LANES :], 1, 1)
    lane = lax.broadcasted_iota(jnp.int32, rest.shape, 1)
    rest_ref[...] = jnp.where(lane >= LANES - (width - whole), rest, 0.0).astype(bf16)
    d_attended = dot(w_out_ref[...], d_branch, 1, 0).astype(bf16)
    for head in range(H):
        part = slice(head * HD, (head + 1) * HD)
        dot_ref[head, :HD, :] = jnp.zeros((HD, rows), bf16)
        dot_ref[head, HD:, :] = d_attended[part]
        delta_ref[head : head + 1, :] = jnp.sum(
            d_attended[part].astype(f32) * att_ref[part, :], axis=0, keepdims=True
        )
    delta_ref[H:, :] = jnp.zeros_like(delta_ref[H:, :])


def mlp(tokens, cot, att, w_out, gain, w_gate, w_up, w_down):
    width, rows = tokens.shape
    hidden_units = w_gate.shape[1]
    vmem = pl.BlockSpec(memory_space=pltpu.VMEM)
    return pl.pallas_call(
        mlp_kernel,
        out_shape=(
            jax.ShapeDtypeStruct((width, rows), bf16),
            jax.ShapeDtypeStruct(
                ((3 * hidden_units + width) // LANES, width, LANES), bf16
            ),
            jax.ShapeDtypeStruct((width, LANES), bf16),
            jax.ShapeDtypeStruct((1, width), f32),
            jax.ShapeDtypeStruct((width, rows), f32),
            jax.ShapeDtypeStruct((H, PAIR, rows), bf16),
            jax.ShapeDtypeStruct((16, rows), f32),
        ),
        in_specs=[vmem] * 8,
        out_specs=(vmem,) * 7,
        compiler_params=pltpu.CompilerParams(vmem_limit_bytes=VMEM_LIMIT),
        name="mlp",
    )(tokens, cot, att, w_out, gain, w_gate, w_up, w_down)


class Reduction:
    def __init__(self, refs, sems, height, rank, row):
        self.source, self.result, self.half, self.from_core, self.from_xy, self.from_z = refs
        self.send, self.recv = sems
        self.height = height
        self.z, self.x = lax.div(rank, 2), lax.rem(rank, 2)
        self.y, self.core = lax.div(row, 2), lax.rem(row, 2)
        self.core_mate = (rank, row + 1 - 2 * self.core)
        self.y_mate = (rank, row + 2 - 4 * self.y)
        self.x_mate = (rank + 1 - 2 * self.x, row)
        self.row = row
        self.split = TILES // 2
        half, quarter = height // 2, height // 4
        self.first_a, self.first_b = half * self.x, half * self.y
        self.other_a, self.other_b = half - self.first_a, half - self.first_b
        self.quarter_a = self.first_a + quarter * self.y
        self.quarter_b = self.first_b + quarter * self.x
        self.across_a = self.first_a + quarter * (1 - self.y)
        self.across_b = self.first_b + quarter * (1 - self.x)

    def copy(self, src, dst, number, phase, slot, there, target):
        return pltpu.make_async_remote_copy(
            src_ref=src,
            dst_ref=dst,
            send_sem=self.send.at[number, phase, slot],
            recv_sem=self.recv.at[number, phase, there],
            device_id=target,
            device_id_type=MESH,
        )

    def rows(self, first, parts):
        return pl.ds(pl.multiple_of(first, 16), self.height // parts)

    def tiles(self, number, core):
        return pl.ds(number * 2 * TILES + core * TILES, TILES)

    def quarter_of(self, tile):
        return jnp.where(tile < self.split, self.quarter_a, self.quarter_b)

    def copies(self, number, phase):
        head, tail = pl.ds(0, self.split), pl.ds(self.split, TILES - self.split)
        base = number * 2 * TILES + self.core * TILES
        out_head = pl.ds(base, self.split)
        out_tail = pl.ds(base + self.split, TILES - self.split)
        if phase == 0:
            src = self.source.at[self.tiles(number, 1 - self.core)]
            dst = self.from_core.at[number]
            return [self.copy(src, dst, number, 0, 0, 0, self.core_mate)]
        if phase in (1, 2):
            parts = 2 * phase
            row_a = self.rows(self.other_a if phase == 1 else self.across_a, parts)
            row_b = self.rows(self.other_b if phase == 1 else self.across_b, parts)
            size = self.height // parts
            first = 0 if phase == 1 else self.height // 2
            mates = (self.x_mate, self.y_mate) if phase == 1 else (self.y_mate, self.x_mate)
            return [
                self.copy(
                    self.half.at[number, part, row],
                    self.from_xy.at[number, part, pl.ds(first, size)],
                    number,
                    phase,
                    slot,
                    slot,
                    mates[slot],
                )
                for slot, (part, row) in enumerate(((head, row_a), (tail, row_b)))
            ]
        if phase in (3, 4):
            made = []
            for step in range(1, TILES):
                other = lax.rem(self.z + step, TILES)
                target = (2 * other + self.x, self.row)
                if phase == 3:
                    src = self.half.at[number, other, self.rows(self.quarter_of(other), 4)]
                    dst = self.from_z.at[number, self.z]
                else:
                    src = self.result.at[base + self.z, self.rows(self.quarter_of(self.z), 4)]
                    dst = src
                made.append(self.copy(src, dst, number, phase, other, self.z, target))
            return made
        if phase in (5, 6):
            parts = 4 if phase == 5 else 2
            row_a = self.rows(self.quarter_a if phase == 5 else self.first_a, parts)
            row_b = self.rows(self.quarter_b if phase == 5 else self.first_b, parts)
            mates = (self.y_mate, self.x_mate) if phase == 5 else (self.x_mate, self.y_mate)
            return [
                self.copy(
                    self.result.at[part, row],
                    self.result.at[part, row],
                    number,
                    phase,
                    slot,
                    slot,
                    mates[slot],
                )
                for slot, (part, row) in enumerate(((out_head, row_a), (out_tail, row_b)))
            ]
        place = self.result.at[self.tiles(number, self.core)]
        return [self.copy(place, place, number, 7, 0, 0, self.core_mate)]

    def arrivals(self, number, phase):
        if phase not in (3, 4):
            return self.copies(number, phase)
        made = []
        base = number * 2 * TILES + self.core * TILES
        for step in range(1, TILES):
            other = lax.rem(self.z + step, TILES)
            target = (2 * other + self.x, self.row)
            if phase == 3:
                dst = self.from_z.at[number, other]
            else:
                dst = self.result.at[base + other, self.rows(self.quarter_of(other), 4)]
            made.append(self.copy(dst, dst, number, phase, other, other, target))
        return made

    def start(self, number, phase):
        for made in self.copies(number, phase):
            made.start()

    def finish(self, number, phase):
        for made in self.arrivals(number, phase):
            made.wait_recv()
        head, tail = pl.ds(0, self.split), pl.ds(self.split, TILES - self.split)
        if phase == 0:
            own = self.source[self.tiles(number, self.core)].astype(f32)
            self.half[number] = (own + self.from_core[number].astype(f32)).astype(bf16)
        if phase in (1, 2):
            parts = 2 * phase
            size = self.height // parts
            first = 0 if phase == 1 else self.height // 2
            row_a = self.rows(self.first_a if phase == 1 else self.quarter_a, parts)
            row_b = self.rows(self.first_b if phase == 1 else self.quarter_b, parts)
            for part, row in ((head, row_a), (tail, row_b)):
                other = self.from_xy[number, part, first : first + size].astype(f32)
                own = self.half[number, part, row].astype(f32)
                self.half[number, part, row] = (own + other).astype(bf16)
        if phase == 3:
            row = self.rows(self.quarter_of(self.z), 4)
            total = self.half[number, self.z, row].astype(f32)
            for step in range(1, TILES):
                other = lax.rem(self.z + step, TILES)
                total = total + self.from_z[number, other].astype(f32)
            base = number * 2 * TILES + self.core * TILES
            self.result[base + self.z, row] = total.astype(bf16)

    def event(self, number, phase):
        if phase > 0:
            self.finish(number, phase - 1)
        if phase < 8:
            self.start(number, phase)

    def drain(self, number):
        for phase in range(8):
            for made in self.copies(number, phase):
                made.wait_send()


def reduction_scratch(numbers, height):
    dma = pltpu.SemaphoreType.DMA
    return [
        pltpu.VMEM((numbers, TILES, height, LANES), bf16),
        pltpu.VMEM((numbers, TILES, height, LANES), bf16),
        pltpu.VMEM((numbers, TILES, height * 3 // 4, LANES), bf16),
        pltpu.VMEM((numbers, TILES, height // 4, LANES), bf16),
        dma((numbers, 8, TILES)),
        dma((numbers, 8, TILES)),
    ]


def back_kernel(
    ranks,
    reduce_here,
    tokens_ref,
    seg_ref,
    gain_ref,
    wq_ref,
    wk_ref,
    wv_ref,
    table_ref,
    qt_ref,
    kv_ref,
    lse_ref,
    dot_ref,
    delta_ref,
    d_middle_ref,
    source_ref,
    rest_ref,
    gain_mlp_ref,
    out_ref,
    grads_ref,
    late_ref,
    turn_ref,
    bias_ref,
    acc_ref,
    d_all_ref,
    terms_ref,
    off_out_ref,
    off_in_ref,
    z_out_ref,
    z_in_ref,
    turn_sem,
    off_send,
    off_recv,
    z_send,
    z_recv,
    *reduction_refs,
):
    rank = lax.axis_index("seq")
    row = lax.axis_index("batch")
    width, rows = tokens_ref.shape
    levels = ranks // 2
    depth = lax.div(rank, 2)
    odd = lax.rem(rank, 2)
    mate = rank + 1 - 2 * odd

    turn_copy = pltpu.make_async_copy(table_ref.at[rank], turn_ref, turn_sem)
    turn_copy.start()
    barrier = pltpu.get_barrier_semaphore()
    peers = [(mate, row)]
    for step in range(1, levels):
        peers.append((2 * lax.rem(depth + step, levels) + odd, row))
    if reduce_here:
        core = lax.rem(row, 2)
        peers.append((rank, row + 1 - 2 * core))
        peers.append((rank, row + 2 - 4 * lax.div(row, 2)))
    for peer in peers:
        pl.semaphore_signal(barrier, inc=1, device_id=peer, device_id_type=MESH)
    pl.semaphore_wait(barrier, len(peers))

    schedule = {}
    after_loop = []
    rounds = 0
    if reduce_here:
        early_scratch, late_scratch = reduction_refs[:6], reduction_refs[6:12]
        late_source = reduction_refs[12]
        rounds = source_ref.shape[0] // (2 * TILES)
        early = Reduction(
            (source_ref, grads_ref) + early_scratch[:4], early_scratch[4:], width, rank, row
        )
        last = Reduction(
            (late_source, late_ref) + late_scratch[:4],
            late_scratch[4:],
            width + EXTRA,
            rank,
            row,
        )
        for number in range(rounds):
            early.start(number, 0)
        for diagonal in range(1, rounds + 8):
            events = [
                (number, diagonal - number)
                for number in range(rounds)
                if 1 <= diagonal - number <= 8
            ]
            place = 1 + SPACING * (diagonal - 1)
            if place < KVH * ranks:
                schedule[place] = events
            else:
                after_loop.append(events)
    else:
        late_source = late_ref

    seg_row = seg_ref[...]
    in_long = long_row(seg_row)
    acc_ref[...] = jnp.zeros_like(acc_ref)

    def off_copy(slot, group):
        return pltpu.make_async_remote_copy(
            src_ref=off_out_ref.at[slot, group],
            dst_ref=off_in_ref.at[slot, group],
            send_sem=off_send.at[slot, group],
            recv_sem=off_recv.at[slot, group],
            device_id=(mate, row),
            device_id_type=MESH,
        )

    def z_copy(slot, group):
        return pltpu.make_async_remote_copy(
            src_ref=z_out_ref.at[slot, group],
            dst_ref=z_in_ref.at[slot, group],
            send_sem=z_send.at[slot, group],
            recv_sem=z_recv.at[slot, group],
            device_id=(rank - 2, row),
            device_id_type=MESH,
        )

    def pair_step(block, group, masked):
        pair = kv_ref[block, group, :rows, :]
        keys_t = pair.T[:HD]
        heads = range(group * GROUP, (group + 1) * GROUP)
        old = [acc_ref[head] for head in heads]
        total = jnp.zeros((rows, PAIR), f32)
        results = []
        for spot, head in enumerate(heads):
            scores = dot(pair, qt_ref[head], 1, 0)
            level = lse_ref[head : head + 1, :]
            if masked:
                scores = scores + bias_ref[...]
            else:
                level = jnp.where(in_long, level, never)
            probs = jnp.exp2(scores - level)
            d_probs = dot(pair, dot_ref[head], 1, 0)
            d_scores = (probs * (d_probs - delta_ref[head : head + 1, :])).astype(bf16)
            total = total + dot(probs.astype(bf16), dot_ref[head], 1, 1)
            total = total + dot(d_scores, qt_ref[head], 1, 1)
            results.append(old[spot] + dot(keys_t, d_scores, 1, 0))
        for spot, head in enumerate(heads):
            acc_ref[head] = results[spot]
        slot = lax.div(block, 2)
        straight = lax.rem(block, 2) == odd
        low = total.astype(bf16)

        @pl.when(straight)
        def _():
            terms_ref[slot, group] = low

        @pl.when(jnp.logical_not(straight))
        def _():
            off_out_ref[slot, group] = low
            off_copy(slot, group).start()

    def combine(time):
        block = time - (levels - depth)
        valid = (block >= 0) & (block <= rank) & (lax.rem(block + 2 * levels, 2) == odd)
        slot = lax.div(jnp.maximum(block, 0), 2)
        from_mate = valid & (mate > block)
        from_above = valid & (depth < levels - 1)
        owner = valid & (block == rank)
        for group in range(KVH):

            @pl.when(from_mate)
            def _():
                off_copy(slot, group).wait_recv()

            @pl.when(from_above)
            def _():
                z_copy(slot, group).wait_recv()

            @pl.when(valid)
            def _():
                total = terms_ref[slot, group].astype(f32)
                total = total + jnp.where(from_mate, off_in_ref[slot, group].astype(f32), 0.0)
                total = total + jnp.where(from_above, z_in_ref[slot, group].astype(f32), 0.0)
                z_out_ref[slot, group] = total.astype(bf16)

            @pl.when(valid & jnp.logical_not(owner))
            def _():
                z_copy(slot, group).start()

    def step(block, carry):
        @pl.when((block == 0) & (rank > 0))
        def _():
            key_bias = first_bias(kv_ref[0, 0, rows:, :], rows)
            bias_ref[...] = key_bias + jnp.where(in_long, 0.0, masked_value)

        @pl.when(block == rank)
        def _():
            bias_ref[...] = own_bias(seg_row)

        masked = (block == 0) | (block == rank)
        for group in range(KVH):

            @pl.when(masked)
            def _():
                pair_step(block, group, True)

            @pl.when(jnp.logical_not(masked) & (block < rank))
            def _():
                pair_step(block, group, False)

            for place, events in schedule.items():
                if place % KVH == group:

                    @pl.when(block == place // KVH)
                    def _():
                        for number, phase in events:
                            early.event(number, phase)

        combine(block)
        return carry

    lax.fori_loop(0, ranks, step, 0)
    combine(ranks)

    turn_copy.wait()
    cosine = turn_ref[: HD // 2]
    sine = turn_ref[HD // 2 :]
    q_cols, k_cols = H * HD, KVH * HD
    for head in range(H):
        turned = turn_back(acc_ref[head] * HD**-0.5, cosine, sine)
        d_all_ref[head * HD : (head + 1) * HD, :] = turned.astype(bf16)
    for group in range(KVH):
        both = z_out_ref[depth, group].astype(f32).T
        first = q_cols + group * HD
        turned = turn_back(both[:HD] * LN2, cosine, sine)
        d_all_ref[first : first + HD, :] = turned.astype(bf16)
        d_all_ref[first + k_cols : first + k_cols + HD, :] = both[HD:].astype(bf16)
    used = q_cols + 2 * k_cols
    d_all_ref[used:, :] = jnp.zeros((d_all_ref.shape[0] - used, rows), bf16)
    inverse, scaled = norm_parts(tokens_ref[...].astype(f32))
    gain = column(gain_ref[...], width)
    normed_t = (scaled * gain).astype(bf16)
    d_normed = (
        dot(wq_ref[...], d_all_ref[:q_cols], 1, 0)
        + dot(wk_ref[...], d_all_ref[q_cols : q_cols + k_cols], 0, 0)
        + dot(wv_ref[...], d_all_ref[q_cols + k_cols : used], 0, 0)
    )
    gain_attn = jnp.sum(d_normed * scaled, axis=1, keepdims=True)
    gain_attn = jnp.broadcast_to(gain_attn, (width, LANES)).T[:1]
    spot = lax.broadcasted_iota(jnp.int32, (EXTRA, LANES), 0)
    for tile in range(2 * TILES):
        part = slice(tile * LANES, (tile + 1) * LANES)
        grad = dot(normed_t, d_all_ref[part], 1, 1)
        if tile == 2 * TILES - 1:
            grad = grad + rest_ref[...].astype(f32)
        late_source[tile, :width, :] = grad.astype(bf16)
        left = min(width - tile * LANES, LANES)
        if left > 0:
            chosen = slice(tile * LANES, tile * LANES + left)
            pad = jnp.zeros((1, LANES - left), f32)
            first, second = gain_attn[:, chosen], gain_mlp_ref[:, chosen]
            if left < LANES:
                first = jnp.concatenate([first, pad], axis=1)
                second = jnp.concatenate([second, pad], axis=1)
            extra = jnp.where(spot == 0, first, jnp.where(spot == 1, second, 0.0))
        else:
            extra = jnp.zeros((EXTRA, LANES), f32)
        late_source[tile, width:, :] = extra.astype(bf16)

    if reduce_here:
        last.start(0, 0)
    mixed = d_normed * gain
    out_ref[...] = d_middle_ref[...] + inverse * (
        mixed - scaled * jnp.mean(mixed * scaled, axis=0, keepdims=True)
    )
    if reduce_here:
        for phase in range(1, 9):
            if after_loop:
                for number, early_phase in after_loop.pop(0):
                    early.event(number, early_phase)
            last.event(0, phase)
        for events in after_loop:
            for number, early_phase in events:
                early.event(number, early_phase)
        for number in range(rounds):
            early.drain(number)
        last.drain(0)
    else:
        grads_ref[...] = source_ref[...]

    def sent(block, carry):
        slot = lax.div(block, 2)
        straight = lax.rem(block, 2) == odd
        for group in range(KVH):

            @pl.when(jnp.logical_not(straight))
            def _():
                off_copy(slot, group).wait_send()

            @pl.when(straight & (block < rank))
            def _():
                z_copy(slot, group).wait_send()

        return carry

    lax.fori_loop(0, rank + 1, sent, 0)


def back(
    ranks,
    reduce_here,
    tokens,
    seg_row,
    gain,
    wq,
    wk,
    wv,
    qt,
    kv,
    lse,
    dot_t,
    delta,
    d_middle,
    grads,
    rest,
    gain_mlp,
):
    width, rows = tokens.shape
    levels = ranks // 2
    vmem = pl.BlockSpec(memory_space=pltpu.VMEM)
    table = jnp.asarray(angle_table(ranks, rows))
    dma = pltpu.SemaphoreType.DMA
    late_shape = (2 * TILES, width + EXTRA, LANES)
    scratch = [
        pltpu.VMEM((HD, rows), f32),
        pltpu.VMEM((rows, rows), f32),
        pltpu.VMEM((H, HD, rows), f32),
        pltpu.VMEM((2 * TILES * LANES, rows), bf16),
    ]
    scratch += [pltpu.VMEM((levels, KVH, rows, PAIR), bf16)] * 5
    scratch += [dma(())] + [dma((levels, KVH))] * 4
    if reduce_here:
        scratch += reduction_scratch(grads.shape[0] // (2 * TILES), width)
        scratch += reduction_scratch(1, width + EXTRA)
        scratch += [pltpu.VMEM(late_shape, bf16)]
    return pl.pallas_call(
        functools.partial(back_kernel, ranks, reduce_here),
        out_shape=(
            jax.ShapeDtypeStruct((width, rows), f32),
            jax.ShapeDtypeStruct(grads.shape, bf16),
            jax.ShapeDtypeStruct(late_shape, bf16),
        ),
        in_specs=[vmem] * 6 + [pl.BlockSpec(memory_space=pl.ANY)] + [vmem] * 9,
        out_specs=(vmem,) * 3,
        scratch_shapes=scratch,
        compiler_params=pltpu.CompilerParams(
            collective_id=1, has_side_effects=True, vmem_limit_bytes=VMEM_LIMIT
        ),
        name="back",
    )(
        tokens,
        seg_row,
        gain,
        wq,
        wk,
        wv,
        table,
        qt,
        kv,
        lse,
        dot_t,
        delta,
        d_middle,
        grads,
        rest,
        gain_mlp,
    )


def finish_kernel(
    gate_ref,
    up_ref,
    down_ref,
    grads_ref,
    late_ref,
    d_inputs_ref,
    gain_attn_ref,
    query_ref,
    key_ref,
    value_ref,
    out_ref,
    gain_mlp_ref,
    grad_gate_ref,
    grad_up_ref,
    grad_down_ref,
    d_tokens_ref,
):
    width = query_ref.shape[0]
    d_tokens_ref[...] = d_inputs_ref[...]
    for tile in range(gate_ref.shape[0]):
        part = slice(tile * LANES, (tile + 1) * LANES)
        grad_gate_ref[:, part] = gate_ref[tile].astype(f32)
        grad_up_ref[:, part] = up_ref[tile].astype(f32)
        grad_down_ref[:, part] = down_ref[tile].astype(f32)

    @pl.when(pl.program_id(0) == 0)
    def _():
        late = jnp.concatenate(
            [late_ref[tile, :width, :].astype(f32) for tile in range(2 * TILES)], axis=1
        )
        q_cols, k_cols = H * HD, KVH * HD
        used = q_cols + 2 * k_cols
        query_ref[...] = late[:, :q_cols]
        key_ref[...] = late[:, q_cols : q_cols + k_cols].T
        value_ref[...] = late[:, q_cols + k_cols : used].T
        whole = grads_ref.shape[0]
        for tile in range(whole):
            out_ref[:, tile * LANES : (tile + 1) * LANES] = grads_ref[tile].astype(f32)
        out_ref[:, whole * LANES :] = late[:, used : used + width - whole * LANES]
        extra = [
            late_ref[tile, width : width + 16, :].astype(f32)
            for tile in range(-(-width // LANES))
        ]
        extra = jnp.concatenate(extra, axis=1)
        gain_attn_ref[...] = extra[0, :width]
        gain_mlp_ref[...] = extra[1, :width]


def finish(grads, late, d_inputs, hidden_units):
    tiles = hidden_units // LANES
    steps = FINISH_STEPS
    width, rows = d_inputs.shape
    each = tiles // steps
    whole = width // LANES
    fixed = lambda shape: pl.BlockSpec(shape, lambda i: (0,) * len(shape))
    tile_at = lambda base: pl.BlockSpec((each, width, LANES), lambda i: (base * steps + i, 0, 0))
    k_cols = KVH * HD
    return pl.pallas_call(
        finish_kernel,
        grid=(steps,),
        out_shape=(
            jax.ShapeDtypeStruct((width,), f32),
            jax.ShapeDtypeStruct((width, H * HD), f32),
            jax.ShapeDtypeStruct((k_cols, width), f32),
            jax.ShapeDtypeStruct((k_cols, width), f32),
            jax.ShapeDtypeStruct((H * HD, width), f32),
            jax.ShapeDtypeStruct((width,), f32),
            jax.ShapeDtypeStruct((width, hidden_units), f32),
            jax.ShapeDtypeStruct((width, hidden_units), f32),
            jax.ShapeDtypeStruct((width, hidden_units), f32),
            jax.ShapeDtypeStruct((width, rows), f32),
        ),
        in_specs=[
            tile_at(0),
            tile_at(1),
            tile_at(2),
            pl.BlockSpec((whole, width, LANES), lambda i: (3 * tiles // whole, 0, 0)),
            fixed(late.shape),
            pl.BlockSpec((width // steps, rows), lambda i: (i, 0)),
        ],
        out_specs=(
            fixed((width,)),
            fixed((width, H * HD)),
            fixed((k_cols, width)),
            fixed((k_cols, width)),
            fixed((H * HD, width)),
            fixed((width,)),
        )
        + (pl.BlockSpec((width, each * LANES), lambda i: (0, i)),) * 3
        + (pl.BlockSpec((width // steps, rows), lambda i: (i, 0)),),
        compiler_params=pltpu.CompilerParams(vmem_limit_bytes=VMEM_LIMIT),
        name="finish",
    )(grads, grads, grads, grads, late, d_inputs)


def local(
    ranks,
    batches,
    tokens,
    segment_ids,
    gain_attn,
    w_query,
    w_key,
    w_value,
    w_out,
    gain_mlp,
    w_gate,
    w_up,
    w_down,
    cotangent,
):
    tokens_t, cot_t = tokens[0].T, cotangent[0].T
    w_key_t, w_value_t, w_down_t = w_key.T, w_value.T, w_down.T
    both_axes = ("seq", "batch")
    qt, kv, att, lse = attend(
        tokens_t, segment_ids, gain_attn, w_query, w_key_t, w_value_t, ranks
    )
    output, grads, rest, grad_gain_mlp, d_middle, dot_t, delta = mlp(
        tokens_t, cot_t, att, w_out, gain_mlp, w_gate, w_up, w_down_t
    )
    reduce_here = ranks == 2 * TILES and batches == 4
    d_inputs, reduced, late = back(
        ranks,
        reduce_here,
        tokens_t,
        segment_ids,
        gain_attn,
        w_query,
        w_key_t,
        w_value_t,
        qt,
        kv,
        lse,
        dot_t,
        delta,
        d_middle,
        grads if reduce_here else rest[None],
        rest,
        grad_gain_mlp,
    )
    if not reduce_here:
        reduced, late = lax.psum((grads, late), both_axes)
    (
        grad_gain_attn,
        grad_query,
        grad_key,
        grad_value,
        grad_out,
        grad_gain_mlp,
        grad_gate,
        grad_up,
        grad_down,
        d_tokens,
    ) = finish(reduced, late, d_inputs, w_gate.shape[1])
    return (
        output.T[None],
        d_tokens.T[None],
        grad_gain_attn,
        grad_query,
        grad_key.T,
        grad_value.T,
        grad_out,
        grad_gain_mlp,
        grad_gate,
        grad_up,
        grad_down.T,
    )


def solution(mesh):
    split = P("batch", "seq", None)
    return jax.shard_map(
        functools.partial(local, mesh.shape["seq"], mesh.shape["batch"]),
        mesh=mesh,
        in_specs=(split, P("batch", "seq")) + (P(),) * 9 + (split,),
        out_specs=(split, split) + (P(),) * 9,
        check_vma=False,
    )
```

```python
import functools

import jax
import jax.numpy as jnp
import numpy as np
from jax import lax
from jax.experimental import pallas as pl
from jax.experimental.pallas import tpu as pltpu
from jax.sharding import PartitionSpec as P

H = 9
KVH = 3
HD = 64
GROUP = H // KVH
PAIR = 2 * HD
META = 16
LANES = 128
TILES = 4
EXTRA = 64
BACK_POINT = 4
READY = (0, 1, 1, 2, 3)
PACE = (0, 1, 2, 3, 4, 5, 6, 7, 8, 9, 10, 11)
FINISH_STEPS = 6
QUERY_PARTS = 2
FF_CHUNK = 512
LAG = 1
CROSSING = 2
HEAD_TILES = (0, 1, 0, 1, 0)
LATE_HEAD_TILES = (2,)

epsilon = 1e-05
theta_base = 10000.0
masked_value = -1e30
never = 1e30
LOG2E = 1.4426950408889634
LN2 = 0.6931471805599453
MESH = pl.DeviceIdType.MESH
f32 = jnp.float32
bf16 = jnp.bfloat16
VMEM_LIMIT = 62 * 2**20


def dot(left, right, left_dim, right_dim):
    return lax.dot_general(
        left,
        right,
        (((left_dim,), (right_dim,)), ((), ())),
        preferred_element_type=f32,
    )


def angle_table(ranks, rows):
    half = HD // 2
    freqs = theta_base ** (-2.0 * np.arange(half, dtype=np.float64) / HD)
    angles = freqs[:, None] * np.arange(ranks * rows, dtype=np.float64)[None, :]
    table = np.concatenate([np.cos(angles), np.sin(angles)], axis=0).astype(np.float32)
    return np.ascontiguousarray(table.reshape(HD, ranks, rows).transpose(1, 0, 2))


def turn(vectors, cosine, sine):
    half = HD // 2
    first, second = vectors[:half], vectors[half:]
    return jnp.concatenate(
        [first * cosine - second * sine, second * cosine + first * sine], axis=0
    )


def flow(items, first, middle, last, delay):
    ahead = first(items[0])
    behind = []
    for index, item in enumerate(items):
        following = first(items[index + 1]) if index + 1 < len(items) else None
        behind.append((item, middle(item, ahead)))
        if len(behind) > delay:
            last(*behind.pop(0))
        ahead = following
    for entry in behind:
        last(*entry)


def column(vector, rows):
    wide = jnp.broadcast_to(vector.astype(f32).reshape(1, rows), (128, rows))
    return wide.T[:, :1]


def norm_parts(inputs):
    mean = jnp.mean(inputs * inputs, axis=0, keepdims=True)
    inverse = lax.rsqrt(mean + epsilon)
    return inverse, inputs * inverse


def turn_back(vectors, cosine, sine):
    half = HD // 2
    first, second = vectors[:half], vectors[half:]
    return jnp.concatenate(
        [first * cosine + second * sine, second * cosine - first * sine], axis=0
    )


def own_bias(seg_row):
    rows = seg_row.shape[1]
    ids = seg_row.astype(f32)
    columns = jnp.broadcast_to(ids, (128, rows)).T[:, :1]
    key = lax.broadcasted_iota(jnp.int32, (rows, rows), 0)
    query = lax.broadcasted_iota(jnp.int32, (rows, rows), 1)
    visible = (columns == ids) & (key <= query)
    return jnp.where(visible, 0.0, masked_value)


def long_row(seg_row):
    return seg_row == seg_row[:, :1]


def first_bias(meta, rows):
    start = 2.0 * meta[0:1, :1].astype(f32) + meta[1:2, :1].astype(f32)
    key = lax.broadcasted_iota(jnp.int32, (rows, 1), 0).astype(f32)
    return jnp.where(key >= start, 0.0, masked_value)


def greet_peers(ranks, reduce_here):
    rank = lax.axis_index("seq")
    row = lax.axis_index("batch")
    levels = ranks // 2
    depth = lax.div(rank, 2)
    odd = lax.rem(rank, 2)
    barrier = pltpu.get_barrier_semaphore()
    peers = [(rank + 1 - 2 * odd, row)]
    for step in range(1, levels):
        peers.append((2 * lax.rem(depth + step, levels) + odd, row))
    if reduce_here:
        core = lax.rem(row, 2)
        peers.append((rank, row + 1 - 2 * core))
        peers.append((rank, row + 2 - 4 * lax.div(row, 2)))
    for peer in peers:
        pl.semaphore_signal(barrier, inc=1, device_id=peer, device_id_type=MESH)
    return functools.partial(pl.semaphore_wait, barrier, len(peers))


def attend_kernel(
    ranks,
    greet,
    tokens_ref,
    seg_ref,
    gain_ref,
    wq_ref,
    wk_ref,
    wv_ref,
    table_ref,
    qt_ref,
    kv_ref,
    att_ref,
    lse_ref,
    turn_ref,
    max_ref,
    sum_ref,
    turn_sem,
    z_sem,
    x_sem,
    in_sem,
):
    rank = lax.axis_index("seq")
    row = lax.axis_index("batch")
    width, rows = tokens_ref.shape
    depth = lax.div(rank, 2)
    odd = lax.rem(rank, 2)
    mate = rank + 1 - 2 * odd
    has_up = rank + 2 < ranks

    turn_copy = pltpu.make_async_copy(table_ref.at[rank], turn_ref, turn_sem)
    turn_copy.start()

    greeted = greet()

    def z_copy(block, group):
        return pltpu.make_async_remote_copy(
            src_ref=kv_ref.at[block, group],
            dst_ref=kv_ref.at[block, group],
            send_sem=z_sem.at[block, group],
            recv_sem=in_sem.at[block, group],
            device_id=(rank + 2, row),
            device_id_type=MESH,
        )

    def x_copy(block, group):
        return pltpu.make_async_remote_copy(
            src_ref=kv_ref.at[block, group],
            dst_ref=kv_ref.at[block, group],
            send_sem=x_sem.at[block, group],
            recv_sem=in_sem.at[block, group],
            device_id=(mate, row),
            device_id_type=MESH,
        )

    unused, scaled = norm_parts(tokens_ref[...].astype(f32))
    normed = (scaled * column(gain_ref[...], width)).astype(bf16)
    keys = dot(wk_ref[...], normed, 1, 0)
    values = dot(wv_ref[...], normed, 1, 0)
    seg_row = seg_ref[...]
    start = jnp.sum((seg_row != seg_row[:, rows - 1 :]).astype(f32), axis=1, keepdims=True)
    high = jnp.floor(0.5 * start)
    low = start - 2.0 * high
    which = lax.broadcasted_iota(jnp.int32, (META, PAIR), 0)
    meta = jnp.where(which == 0, high, jnp.where(which == 1, low, 0.0)).astype(bf16)
    turn_copy.wait()
    cosine = turn_ref[: HD // 2]
    sine = turn_ref[HD // 2 :]
    for group in range(KVH):
        part = slice(group * HD, group * HD + HD)
        both = jnp.concatenate([turn(keys[part], cosine, sine), values[part]], axis=0)
        kv_ref[rank, group, :rows, :] = both.astype(bf16).T
        kv_ref[rank, group, rows:, :] = meta

    greeted()
    for group in range(KVH):

        @pl.when(odd == 0)
        def _():
            x_copy(rank, group).start()

        @pl.when(has_up)
        def _():
            z_copy(rank, group).start()

    def relay(level, group):
        block = rank - 2 * level
        z_in = pltpu.make_async_remote_copy(
            src_ref=kv_ref.at[block, group],
            dst_ref=kv_ref.at[block, group],
            send_sem=z_sem.at[block, group],
            recv_sem=in_sem.at[block, group],
            device_id=(mate, row),
            device_id_type=MESH,
        )
        z_in.wait_recv()
        x_copy(block, group).start()

        @pl.when(has_up)
        def _():
            z_copy(block, group).start()

    queries = dot(wq_ref[...], normed, 0, 0)
    for head in range(H):
        part = slice(head * HD, head * HD + HD)
        turned = turn(queries[part], cosine, sine) * (LOG2E / HD**0.5)
        qt_ref[head, :HD, :] = turned.astype(bf16)
        qt_ref[head, HD:, :] = jnp.zeros((HD, rows), bf16)

    bias = own_bias(seg_row)
    size = rows // QUERY_PARTS
    items = [(head, part) for head in range(H) for part in range(QUERY_PARTS)]

    def own_scores(item):
        head, part = item
        seen = (part + 1) * size
        across = slice(part * size, seen)
        pair = kv_ref[rank, head // GROUP, :seen, :]
        return dot(pair, qt_ref[head, :, across], 1, 0) + bias[:seen, across]

    def own_weights(item, scores):
        head, part = item
        across = slice(part * size, (part + 1) * size)
        top = jnp.max(scores, axis=0, keepdims=True)
        weights = jnp.exp2(scores - top)
        max_ref[head : head + 1, across] = top
        sum_ref[head : head + 1, across] = jnp.sum(weights, axis=0, keepdims=True)
        return weights.astype(bf16)

    def own_values(item, weights):
        head, part = item
        seen = (part + 1) * size
        across = slice(part * size, seen)
        values_t = kv_ref[rank, head // GROUP, :seen, :].T[HD:]
        att_ref[head * HD : (head + 1) * HD, across] = dot(values_t, weights, 1, 0)

    flow(items, own_scores, own_weights, own_values, 1)

    @pl.when(depth >= 1)
    def _():
        for group in range(KVH):
            relay(1, group)

    in_long = long_row(seg_row)

    def block_step(block, key_bias):
        def scores_of(item):
            head, part = item
            across = slice(part * size, (part + 1) * size)
            pair = kv_ref[block, head // GROUP, :rows, :]
            scores = dot(pair, qt_ref[head, :, across], 1, 0)
            return scores if key_bias is None else scores + key_bias

        def weights_of(item, scores):
            head, part = item
            across = slice(part * size, (part + 1) * size)
            seen = in_long[:, across]
            old = max_ref[head : head + 1, across]
            top = jnp.maximum(old, jnp.max(scores, axis=0, keepdims=True))
            top = jnp.where(seen, top, old)
            weights = jnp.exp2(scores - jnp.where(seen, top, never))
            scale = jnp.exp2(old - top)
            max_ref[head : head + 1, across] = top
            sum_ref[head : head + 1, across] = sum_ref[
                head : head + 1, across
            ] * scale + jnp.sum(weights, axis=0, keepdims=True)
            return scale, weights.astype(bf16)

        def values_of(item, results):
            head, part = item
            scale, weights = results
            across = slice(part * size, (part + 1) * size)
            place = slice(head * HD, (head + 1) * HD)
            values_t = kv_ref[block, head // GROUP, :rows, :].T[HD:]
            att_ref[place, across] = att_ref[place, across] * scale + dot(
                values_t, weights, 1, 0
            )

        flow(items, scores_of, weights_of, values_of, 1)

    def step(index, carry):
        level = lax.div(index + 1, 2)
        straight = lax.rem(index, 2) == 1
        block = jnp.where(straight, rank, mate) - 2 * level

        @pl.when(jnp.logical_not(straight))
        def _():
            for group in range(KVH):
                x_copy(block, group).wait_recv()

        @pl.when(block == 0)
        def _():
            block_step(block, first_bias(kv_ref[0, 0, rows:, :], rows))

        @pl.when(block != 0)
        def _():
            block_step(block, None)

        @pl.when(straight & (level + 1 <= depth))
        def _():
            for group in range(KVH):
                relay(level + 1, group)

        return carry

    lax.fori_loop(1 - odd, 2 * depth + 1, step, 0)

    for head in range(H):
        part = slice(head * HD, (head + 1) * HD)
        total = sum_ref[head : head + 1, :]
        att_ref[part, :] = att_ref[part, :] / total
        lse_ref[head : head + 1, :] = max_ref[head : head + 1, :] + jnp.log2(total)
    lse_ref[H:, :] = jnp.zeros_like(lse_ref[H:, :])

    def sent(level, carry):
        block = rank - 2 * level
        for group in range(KVH):

            @pl.when(has_up)
            def _():
                z_copy(block, group).wait_send()

            @pl.when((odd == 0) | (level >= 1))
            def _():
                x_copy(block, group).wait_send()

        return carry

    lax.fori_loop(0, depth + 1, sent, 0)


def attend(tokens, seg_row, gain, wq, wk, wv, ranks):
    width, rows = tokens.shape
    vmem = pl.BlockSpec(memory_space=pltpu.VMEM)
    table = jnp.asarray(angle_table(ranks, rows))
    dma = pltpu.SemaphoreType.DMA
    return pl.pallas_call(
        functools.partial(attend_kernel, ranks, functools.partial(greet_peers, ranks, False)),
        out_shape=(
            jax.ShapeDtypeStruct((H, PAIR, rows), bf16),
            jax.ShapeDtypeStruct((ranks, KVH, rows + META, PAIR), bf16),
            jax.ShapeDtypeStruct((H * HD, rows), f32),
            jax.ShapeDtypeStruct((16, rows), f32),
        ),
        in_specs=[vmem] * 6 + [pl.BlockSpec(memory_space=pl.ANY)],
        out_specs=(vmem,) * 4,
        scratch_shapes=[
            pltpu.VMEM((HD, rows), f32),
            pltpu.VMEM((16, rows), f32),
            pltpu.VMEM((16, rows), f32),
            dma(()),
            dma((ranks, KVH)),
            dma((ranks, KVH)),
            dma((ranks, KVH)),
        ],
        compiler_params=pltpu.CompilerParams(
            collective_id=0, has_side_effects=True, vmem_limit_bytes=VMEM_LIMIT
        ),
        name="attend",
    )(tokens, seg_row, gain, wq, wk, wv, table)


def mlp_kernel(
    reached,
    tokens_ref,
    cot_ref,
    att_ref,
    w_out_ref,
    gain_ref,
    w_gate_ref,
    w_up_ref,
    w_down_ref,
    out_ref,
    grads_ref,
    rest_ref,
    gain_grad_ref,
    d_middle_ref,
    dot_ref,
    delta_ref,
):
    width, rows = tokens_ref.shape
    hidden_units = w_gate_ref.shape[1]
    chunk = FF_CHUNK
    attended = att_ref[...].astype(bf16)
    middle = tokens_ref[...].astype(f32) + dot(w_out_ref[...], attended, 0, 0)
    inverse, scaled = norm_parts(middle)
    gain = column(gain_ref[...], width)
    normed_t = (scaled * gain).astype(bf16)
    normed = normed_t.T
    cot_t = cot_ref[...]
    cot = cot_t.T
    result = middle
    d_normed = jnp.zeros((width, rows), f32)

    def put_tiles(first, grad):
        for tile in range(grad.shape[1] // LANES):
            part = grad[:, tile * LANES : (tile + 1) * LANES]
            grads_ref[first // LANES + tile] = part.astype(bf16)

    for first in range(0, hidden_units, chunk):
        part = slice(first, first + chunk)
        gate = dot(normed, w_gate_ref[:, part], 1, 0)
        up = dot(normed, w_up_ref[:, part], 1, 0)
        d_hidden = dot(cot, w_down_ref[:, part], 1, 0)
        sigmoid = jax.nn.sigmoid(gate)
        silu = gate * sigmoid
        hidden = (silu * up).astype(bf16)
        d_gate = (d_hidden * up * (sigmoid + silu * (1.0 - sigmoid))).astype(bf16)
        d_up = (d_hidden * silu).astype(bf16)
        result = result + dot(w_down_ref[:, part], hidden, 1, 1)
        d_normed = d_normed + dot(w_gate_ref[:, part], d_gate, 1, 1)
        d_normed = d_normed + dot(w_up_ref[:, part], d_up, 1, 1)
        put_tiles(3 * first, dot(normed_t, d_gate, 1, 0))
        put_tiles(3 * first + chunk, dot(normed_t, d_up, 1, 0))
        put_tiles(3 * first + 2 * chunk, dot(cot_t, hidden, 1, 0))
        reached(first // chunk)
    out_ref[...] = result.astype(bf16)
    gain_grad = jnp.sum(d_normed * scaled, axis=1, keepdims=True)
    gain_grad_ref[...] = jnp.broadcast_to(gain_grad, (width, LANES)).T[:1]
    mixed = d_normed * gain
    d_middle = cot_t.astype(f32) + inverse * (
        mixed - scaled * jnp.mean(mixed * scaled, axis=0, keepdims=True)
    )
    d_middle_ref[...] = d_middle
    d_branch = d_middle.astype(bf16)
    whole = width // LANES * LANES
    put_tiles(3 * hidden_units, dot(attended, d_branch[:whole], 1, 1))
    rest = dot(attended, d_branch[width - LANES :], 1, 1)
    lane = lax.broadcasted_iota(jnp.int32, rest.shape, 1)
    rest_ref[...] = jnp.where(lane >= LANES - (width - whole), rest, 0.0).astype(bf16)
    d_attended = dot(w_out_ref[...], d_branch, 1, 0).astype(bf16)
    for head in range(H):
        part = slice(head * HD, (head + 1) * HD)
        dot_ref[head, :HD, :] = jnp.zeros((HD, rows), bf16)
        dot_ref[head, HD:, :] = d_attended[part]
        delta_ref[head : head + 1, :] = jnp.sum(
            d_attended[part].astype(f32) * att_ref[part, :], axis=0, keepdims=True
        )
    delta_ref[H:, :] = jnp.zeros_like(delta_ref[H:, :])
    reached(hidden_units // chunk)


def mlp(tokens, cot, att, w_out, gain, w_gate, w_up, w_down):
    width, rows = tokens.shape
    hidden_units = w_gate.shape[1]
    vmem = pl.BlockSpec(memory_space=pltpu.VMEM)
    return pl.pallas_call(
        functools.partial(mlp_kernel, lambda point: None),
        out_shape=(
            jax.ShapeDtypeStruct((width, rows), bf16),
            jax.ShapeDtypeStruct(
                ((3 * hidden_units + width) // LANES, width, LANES), bf16
            ),
            jax.ShapeDtypeStruct((width, LANES), bf16),
            jax.ShapeDtypeStruct((1, width), f32),
            jax.ShapeDtypeStruct((width, rows), f32),
            jax.ShapeDtypeStruct((H, PAIR, rows), bf16),
            jax.ShapeDtypeStruct((16, rows), f32),
        ),
        in_specs=[vmem] * 8,
        out_specs=(vmem,) * 7,
        compiler_params=pltpu.CompilerParams(vmem_limit_bytes=VMEM_LIMIT),
        name="mlp",
    )(tokens, cot, att, w_out, gain, w_gate, w_up, w_down)


class Reduction:
    def __init__(self, refs, sems, height, splits, rank, row, plan=None):
        self.plan = dict(plan or {})
        self.source, self.result, self.from_core, self.from_xy, self.from_z = refs
        self.send, self.recv = sems
        self.height = height
        self.z, self.x = lax.div(rank, 2), lax.rem(rank, 2)
        self.y, self.core = lax.div(row, 2), lax.rem(row, 2)
        self.core_mate = (rank, row + 1 - 2 * self.core)
        self.y_mate = (rank, row + 2 - 4 * self.y)
        self.x_mate = (rank + 1 - 2 * self.x, row)
        self.row = row
        self.splits = splits
        half, quarter = height // 2, height // 4
        self.first_a, self.first_b = half * self.x, half * self.y
        self.other_a, self.other_b = half - self.first_a, half - self.first_b
        self.quarter_a = self.first_a + quarter * self.y
        self.quarter_b = self.first_b + quarter * self.x
        self.across_a = self.first_a + quarter * (1 - self.y)
        self.across_b = self.first_b + quarter * (1 - self.x)

    def copy(self, src, dst, number, phase, slot, there, target):
        return pltpu.make_async_remote_copy(
            src_ref=src,
            dst_ref=dst,
            send_sem=self.send.at[number, phase, slot],
            recv_sem=self.recv.at[number, phase, there],
            device_id=target,
            device_id_type=MESH,
        )

    def rows(self, first, parts):
        return pl.ds(pl.multiple_of(first, 16), self.height // parts)

    def tiles(self, number, core):
        return pl.ds(number * 2 * TILES + core * TILES, TILES)

    def quarter_of(self, number, tile):
        return jnp.where(tile < self.splits[number], self.quarter_a, self.quarter_b)

    def ways(self, number, phase):
        split = self.splits[number]
        mates = (self.x_mate, self.y_mate)
        if phase in (2, 5):
            mates = mates[::-1]
        found = []
        for slot, (first, count) in enumerate(((0, split), (split, TILES - split))):
            if count:
                found.append((slot, first, count, mates[slot]))
        return found

    def copies(self, number, phase):
        base = number * 2 * TILES + self.core * TILES
        if phase == 0:
            src = self.source.at[self.tiles(number, 1 - self.core)]
            dst = self.from_core.at[number]
            return [self.copy(src, dst, number, 0, 0, 0, self.core_mate)]
        if phase in (1, 2):
            parts = 2 * phase
            firsts = (self.other_a, self.other_b)
            if phase == 2:
                firsts = (self.across_a, self.across_b)
            size = self.height // parts
            first = 0 if phase == 1 else self.height // 2
            made = []
            for slot, start, count, mate in self.ways(number, phase):
                src = self.source.at[pl.ds(base + start, count), self.rows(firsts[slot], parts)]
                dst = self.from_xy.at[number, pl.ds(start, count), pl.ds(first, size)]
                made.append(self.copy(src, dst, number, phase, slot, slot, mate))
            return made
        if phase in (3, 4):
            made = []
            for step in range(1, TILES):
                other = lax.rem(self.z + step, TILES)
                target = (2 * other + self.x, self.row)
                if phase == 3:
                    src = self.source.at[base + other, self.rows(self.quarter_of(number, other), 4)]
                    dst = self.from_z.at[number, self.z]
                else:
                    src = self.result.at[base + self.z, self.rows(self.quarter_of(number, self.z), 4)]
                    dst = src
                made.append(self.copy(src, dst, number, phase, other, self.z, target))
            return made
        if phase in (5, 6):
            parts = 4 if phase == 5 else 2
            firsts = (self.quarter_a, self.quarter_b)
            if phase == 6:
                firsts = (self.first_a, self.first_b)
            made = []
            for slot, start, count, mate in self.ways(number, phase):
                part = pl.ds(base + start, count)
                place = self.result.at[part, self.rows(firsts[slot], parts)]
                made.append(self.copy(place, place, number, phase, slot, slot, mate))
            return made
        place = self.result.at[self.tiles(number, self.core)]
        return [self.copy(place, place, number, 7, 0, 0, self.core_mate)]

    def arrivals(self, number, phase):
        if phase not in (3, 4):
            return self.copies(number, phase)
        made = []
        base = number * 2 * TILES + self.core * TILES
        for step in range(1, TILES):
            other = lax.rem(self.z + step, TILES)
            target = (2 * other + self.x, self.row)
            if phase == 3:
                dst = self.from_z.at[number, other]
            else:
                dst = self.result.at[base + other, self.rows(self.quarter_of(number, other), 4)]
            made.append(self.copy(dst, dst, number, phase, other, other, target))
        return made

    def start(self, number, phase):
        for made in self.copies(number, phase):
            made.start()

    def finish(self, number, phase):
        for made in self.arrivals(number, phase):
            made.wait_recv()
        base = number * 2 * TILES + self.core * TILES
        if phase == 0:
            mine = self.tiles(number, self.core)
            total = self.source[mine].astype(f32) + self.from_core[number].astype(f32)
            self.source[mine] = total.astype(bf16)
        if phase in (1, 2):
            parts = 2 * phase
            size = self.height // parts
            first = 0 if phase == 1 else self.height // 2
            firsts = (self.first_a, self.first_b)
            if phase == 2:
                firsts = (self.quarter_a, self.quarter_b)
            for slot, start, count, unused in self.ways(number, phase):
                row = self.rows(firsts[slot], parts)
                part = pl.ds(base + start, count)
                other = self.from_xy[number, start : start + count, first : first + size]
                own = self.source[part, row].astype(f32)
                self.source[part, row] = (own + other.astype(f32)).astype(bf16)
        if phase == 3:
            row = self.rows(self.quarter_of(number, self.z), 4)
            total = self.source[base + self.z, row].astype(f32)
            for step in range(1, TILES):
                other = lax.rem(self.z + step, TILES)
                total = total + self.from_z[number, other].astype(f32)
            self.result[base + self.z, row] = total.astype(bf16)

    def event(self, number, phase):
        if phase > 0:
            self.finish(number, phase - 1)
        if phase < 8:
            self.start(number, phase)

    def reach(self, point):
        for when in sorted(self.plan) if point is None else [point]:
            for number, phase in self.plan.pop(when, ()):
                self.event(number, phase)

    def drain(self):
        for number in range(len(self.splits)):
            for phase in range(8):
                for made in self.copies(number, phase):
                    made.wait_send()


def early_plan(rounds):
    plan = {}
    for number in range(rounds):
        for phase in range(9):
            place = max(READY[number], READY[number] + phase, number + phase)
            point = PACE[place] if place < len(PACE) else PACE[-1] + place - len(PACE) + 1
            plan.setdefault(point, []).append((number, phase))
    return plan


def reduction_scratch(numbers, height):
    dma = pltpu.SemaphoreType.DMA
    return [
        pltpu.VMEM((numbers, TILES, height, LANES), bf16),
        pltpu.VMEM((numbers, TILES, height * 3 // 4, LANES), bf16),
        pltpu.VMEM((numbers, TILES, height // 4, LANES), bf16),
        dma((numbers, 8, TILES)),
        dma((numbers, 8, TILES)),
    ]


def back_kernel(
    ranks,
    greet,
    reductions,
    tokens_ref,
    seg_ref,
    gain_ref,
    wq_ref,
    wk_ref,
    wv_ref,
    table_ref,
    qt_ref,
    kv_ref,
    lse_ref,
    dot_ref,
    delta_ref,
    d_middle_ref,
    rest_ref,
    gain_mlp_ref,
    out_ref,
    late_ref,
    turn_ref,
    bias_ref,
    acc_ref,
    d_all_ref,
    terms_ref,
    off_out_ref,
    off_in_ref,
    z_in_ref,
    turn_sem,
    off_send,
    off_recv,
    z_send,
    z_recv,
):
    rank = lax.axis_index("seq")
    row = lax.axis_index("batch")
    width, rows = tokens_ref.shape
    levels = ranks // 2
    depth = lax.div(rank, 2)
    odd = lax.rem(rank, 2)
    mate = rank + 1 - 2 * odd

    turn_copy = None
    if greet is not None:
        turn_copy = pltpu.make_async_copy(table_ref.at[rank], turn_ref, turn_sem)
        turn_copy.start()
        greet()()
    reduce_here = reductions is not None
    if reduce_here:
        early, late, late_source = reductions
    else:
        late_source = late_ref

    crossing = CROSSING if reduce_here else 0
    seg_row = seg_ref[...]
    in_long = long_row(seg_row)
    acc_ref[...] = jnp.zeros_like(acc_ref)

    def off_copy(slot, group):
        return pltpu.make_async_remote_copy(
            src_ref=off_out_ref.at[slot, group],
            dst_ref=off_in_ref.at[slot, group],
            send_sem=off_send.at[slot, group],
            recv_sem=off_recv.at[slot, group],
            device_id=(mate, row),
            device_id_type=MESH,
        )

    def cross_copy(group):
        return pltpu.make_async_remote_copy(
            src_ref=terms_ref.at[levels, group],
            dst_ref=off_in_ref.at[levels, group],
            send_sem=z_send.at[levels, group],
            recv_sem=off_recv.at[levels, group],
            device_id=(mate, row),
            device_id_type=MESH,
        )

    def z_copy(slot, group):
        return pltpu.make_async_remote_copy(
            src_ref=terms_ref.at[slot, group],
            dst_ref=z_in_ref.at[slot, group],
            send_sem=z_send.at[slot, group],
            recv_sem=z_recv.at[slot, group],
            device_id=(rank - 2, row),
            device_id_type=MESH,
        )

    size = rows // QUERY_PARTS

    def pair_step(block, diagonal, masked):
        items = [(head, part) for head in range(H) for part in range(QUERY_PARTS)]
        totals = {}

        def places(part):
            across = slice(part * size, (part + 1) * size)
            return across, (part + 1) * size if diagonal else rows

        def scores_of(item):
            head, part = item
            across, seen = places(part)
            pair = kv_ref[block, head // GROUP, :seen, :]
            scores = dot(pair, qt_ref[head, :, across], 1, 0)
            if masked:
                scores = scores + bias_ref[:seen, across]
            return scores, dot(pair, dot_ref[head, :, across], 1, 0)

        def d_scores_of(item, both):
            head, part = item
            across, seen = places(part)
            scores, d_probs = both
            level = lse_ref[head : head + 1, across]
            if not masked:
                level = jnp.where(in_long[:, across], level, never)
            probs = jnp.exp2(scores - level)
            d_scores = probs * (d_probs - delta_ref[head : head + 1, across])
            return probs.astype(bf16), d_scores.astype(bf16)

        def terms_of(item, both):
            head, part = item
            across, seen = places(part)
            probs, d_scores = both
            group = head // GROUP
            term = dot(dot_ref[head, :, across], probs, 1, 1)
            term = term + dot(qt_ref[head, :, across], d_scores, 1, 1)
            key = (group, seen)
            totals[key] = totals[key] + term if key in totals else term
            keys_t = kv_ref[block, group, :seen, :].T[:HD]
            acc_ref[head, :, across] += dot(keys_t, d_scores, 1, 0)
            if head % GROUP == GROUP - 1 and part == QUERY_PARTS - 1:
                put(group)

        def put(group):
            whole = totals.pop((group, rows))
            rest = totals.pop((group, size), None)
            if rest is not None:
                whole = jnp.concatenate([whole[:, :size] + rest, whole[:, size:]], axis=1)
            low = whole.astype(bf16)
            if diagonal:
                terms_ref[slot_of(block), group] = low
                return
            kept = member(block)

            @pl.when(kept)
            def _():
                terms_ref[slot_of(block), group] = low

            @pl.when(jnp.logical_not(kept))
            def _():
                off_out_ref[lax.div(block, 2), group] = low
                off_copy(lax.div(block, 2), group).start()

        flow(items, scores_of, d_scores_of, terms_of, 1)

    def straight(block):
        return lax.rem(block + 2 * levels, 2) == odd

    def member(block):
        return straight(block) | (block < crossing)

    def slot_of(block):
        slot = lax.div(jnp.maximum(block, 0), 2)
        return jnp.where(straight(block), slot, levels) if crossing else slot

    def combine(time):
        block = time - (levels - depth) - LAG
        owner = block == rank
        over = (block >= 0) & (block < crossing)
        valid = (block >= 0) & (block < 2 * depth + 2) & member(block)
        valid = valid & (owner | (block < rank) | over)
        valid = valid & jnp.logical_not(over & owner)
        gather(block, valid, valid & straight(block) & (mate > block) & jnp.logical_not(over))

        @pl.when(valid & jnp.logical_not(owner) & (depth > lax.div(jnp.maximum(block, 0), 2)))
        def _():
            for group in range(KVH):
                z_copy(slot_of(block), group).start()

        if crossing:

            @pl.when(valid & jnp.logical_not(owner) & (depth == 0))
            def _():
                for group in range(KVH):
                    cross_copy(group).start()

            block = time - 1 - (levels - depth) - LAG
            valid = (block >= 0) & (block < crossing) & (block == rank)
            gather(block, valid, valid, levels)

    def gather(block, valid, from_mate, mate_slot=None):
        slot = slot_of(block)
        if mate_slot is None:
            mate_slot = lax.div(jnp.maximum(block, 0), 2)
        from_above = valid & (depth < levels - 1)
        own = block <= rank
        for group in range(KVH):

            @pl.when(from_mate)
            def _():
                off_copy(mate_slot, group).wait_recv()

            @pl.when(from_above)
            def _():
                z_copy(slot, group).wait_recv()

            @pl.when(valid)
            def _():
                total = jnp.where(own, terms_ref[slot, group].astype(f32), 0.0)
                low = off_in_ref[mate_slot, group].astype(f32)
                total = total + jnp.where(from_mate, low, 0.0)
                low = z_in_ref[slot, group].astype(f32)
                total = total + jnp.where(from_above, low, 0.0)
                terms_ref[slot, group] = total.astype(bf16)

    def step(block, carry):
        @pl.when((block == 0) & (rank > 0))
        def _():
            key_bias = first_bias(kv_ref[0, 0, rows:, :], rows)
            bias_ref[...] = key_bias + jnp.where(in_long, 0.0, masked_value)

        @pl.when(block == rank)
        def _():
            bias_ref[...] = own_bias(seg_row)

        @pl.when(block == rank)
        def _():
            pair_step(block, True, True)

        @pl.when((block == 0) & (rank > 0))
        def _():
            pair_step(block, False, True)

        @pl.when((block > 0) & (block < rank))
        def _():
            pair_step(block, False, False)

        if reduce_here:
            for place in range(ranks):

                @pl.when(block == place)
                def _():
                    early.reach(BACK_POINT + place)

        combine(block)
        return carry

    lax.fori_loop(0, ranks, step, 0)
    for time in range(ranks, ranks + 1 + LAG):
        combine(time)

    if turn_copy is not None:
        turn_copy.wait()
    cosine = turn_ref[: HD // 2]
    sine = turn_ref[HD // 2 :]
    q_cols, k_cols = H * HD, KVH * HD
    for head in range(H):
        turned = turn_back(acc_ref[head] * HD**-0.5, cosine, sine)
        d_all_ref[head * HD : (head + 1) * HD, :] = turned.astype(bf16)
    for group in range(KVH):
        both = terms_ref[depth, group].astype(f32)
        first = q_cols + group * HD
        turned = turn_back(both[:HD] * LN2, cosine, sine)
        d_all_ref[first : first + HD, :] = turned.astype(bf16)
        d_all_ref[first + k_cols : first + k_cols + HD, :] = both[HD:].astype(bf16)
    used = q_cols + 2 * k_cols
    d_all_ref[used:, :] = jnp.zeros((d_all_ref.shape[0] - used, rows), bf16)
    inverse, scaled = norm_parts(tokens_ref[...].astype(f32))
    gain = column(gain_ref[...], width)
    normed_t = (scaled * gain).astype(bf16)
    d_normed = (
        dot(wq_ref[...], d_all_ref[:q_cols], 1, 0)
        + dot(wk_ref[...], d_all_ref[q_cols : q_cols + k_cols], 0, 0)
        + dot(wv_ref[...], d_all_ref[q_cols + k_cols : used], 0, 0)
    )
    gain_attn = jnp.sum(d_normed * scaled, axis=1, keepdims=True)
    gain_attn = jnp.broadcast_to(gain_attn, (width, LANES)).T[:1]
    spot = lax.broadcasted_iota(jnp.int32, (EXTRA, LANES), 0)
    for tile in range(2 * TILES):
        part = slice(tile * LANES, (tile + 1) * LANES)
        grad = dot(normed_t, d_all_ref[part], 1, 1)
        if tile == 2 * TILES - 1:
            grad = grad + rest_ref[...].astype(f32)
        late_source[tile, :width, :] = grad.astype(bf16)
        left = min(width - tile * LANES, LANES)
        if left > 0:
            chosen = slice(tile * LANES, tile * LANES + left)
            pad = jnp.zeros((1, LANES - left), f32)
            first, second = gain_attn[:, chosen], gain_mlp_ref[:, chosen]
            if left < LANES:
                first = jnp.concatenate([first, pad], axis=1)
                second = jnp.concatenate([second, pad], axis=1)
            extra = jnp.where(spot == 0, first, jnp.where(spot == 1, second, 0.0))
        else:
            extra = jnp.zeros((EXTRA, LANES), f32)
        late_source[tile, width:, :] = extra.astype(bf16)

    if reduce_here:
        late.start(0, 0)
    mixed = d_normed * gain
    out_ref[...] = d_middle_ref[...] + inverse * (
        mixed - scaled * jnp.mean(mixed * scaled, axis=0, keepdims=True)
    )
    if reduce_here:
        for phase in range(1, 9):
            early.reach(BACK_POINT + ranks + phase - 1)
            late.event(0, phase)
        early.reach(None)
        early.drain()
        late.drain()

    def sent(block, carry):
        kept = member(block)
        for group in range(KVH):

            @pl.when(jnp.logical_not(kept))
            def _():
                off_copy(lax.div(block, 2), group).wait_send()

            @pl.when(kept & (lax.div(block, 2) < depth))
            def _():
                z_copy(slot_of(block), group).wait_send()

        return carry

    lax.fori_loop(0, rank + 1, sent, 0)
    if crossing:

        @pl.when(depth == 0)
        def _():
            for group in range(KVH):
                cross_copy(group).wait_send()


def back_scratch(ranks, rows, crossing):
    dma = pltpu.SemaphoreType.DMA
    slots = ranks // 2 + (1 if crossing else 0)
    return (
        [
            pltpu.VMEM((rows, rows), f32),
            pltpu.VMEM((H, HD, rows), f32),
            pltpu.VMEM((2 * TILES * LANES, rows), bf16),
        ]
        + [pltpu.VMEM((slots, KVH, PAIR, rows), bf16)] * 4
        + [dma(())]
        + [dma((slots, KVH))] * 4
    )


def back(
    ranks,
    tokens,
    seg_row,
    gain,
    wq,
    wk,
    wv,
    qt,
    kv,
    lse,
    dot_t,
    delta,
    d_middle,
    rest,
    gain_mlp,
):
    width, rows = tokens.shape
    vmem = pl.BlockSpec(memory_space=pltpu.VMEM)
    table = jnp.asarray(angle_table(ranks, rows))
    late_shape = (2 * TILES, width + EXTRA, LANES)
    greet = functools.partial(greet_peers, ranks, False)
    return pl.pallas_call(
        functools.partial(back_kernel, ranks, greet, None),
        out_shape=(
            jax.ShapeDtypeStruct((width, rows), f32),
            jax.ShapeDtypeStruct(late_shape, bf16),
        ),
        in_specs=[vmem] * 6 + [pl.BlockSpec(memory_space=pl.ANY)] + [vmem] * 8,
        out_specs=(vmem,) * 2,
        scratch_shapes=[pltpu.VMEM((HD, rows), f32)] + back_scratch(ranks, rows, False),
        compiler_params=pltpu.CompilerParams(
            collective_id=1, has_side_effects=True, vmem_limit_bytes=VMEM_LIMIT
        ),
        name="back",
    )(
        tokens,
        seg_row,
        gain,
        wq,
        wk,
        wv,
        table,
        qt,
        kv,
        lse,
        dot_t,
        delta,
        d_middle,
        rest,
        gain_mlp,
    )


def layer_kernel(
    ranks,
    tokens_ref,
    seg_ref,
    gain_attn_ref,
    gain_mlp_ref,
    wq_ref,
    wk_ref,
    wv_ref,
    table_ref,
    cot_hbm,
    w_out_hbm,
    w_gate_hbm,
    w_up_hbm,
    w_down_hbm,
    out_ref,
    d_inputs_ref,
    grads_ref,
    late_ref,
    cot_ref,
    w_out_ref,
    w_gate_ref,
    w_up_ref,
    w_down_ref,
    load_sem,
    turn_ref,
    qt_ref,
    kv_ref,
    att_ref,
    lse_ref,
    max_ref,
    sum_ref,
    turn_sem,
    z_sem,
    x_sem,
    in_sem,
    source_ref,
    rest_ref,
    gain_grad_ref,
    d_middle_ref,
    dot_ref,
    delta_ref,
    late_source_ref,
    *others,
):
    rank = lax.axis_index("seq")
    row = lax.axis_index("batch")
    width = tokens_ref.shape[0]
    loads = [
        pltpu.make_async_copy(src, dst, load_sem.at[index])
        for index, (src, dst) in enumerate(
            (
                (cot_hbm, cot_ref),
                (w_out_hbm, w_out_ref),
                (w_gate_hbm, w_gate_ref),
                (w_up_hbm, w_up_ref),
                (w_down_hbm, w_down_ref),
            )
        )
    ]
    for load in loads:
        load.start()
    attend_kernel(
        ranks,
        functools.partial(greet_peers, ranks, True),
        tokens_ref,
        seg_ref,
        gain_attn_ref,
        wq_ref,
        wk_ref,
        wv_ref,
        table_ref,
        qt_ref,
        kv_ref,
        att_ref,
        lse_ref,
        turn_ref,
        max_ref,
        sum_ref,
        turn_sem,
        z_sem,
        x_sem,
        in_sem,
    )
    for load in loads:
        load.wait()
    early_scratch, late_scratch, chain = others[:5], others[5:10], others[10:]
    early = Reduction(
        (source_ref, grads_ref) + early_scratch[:3],
        early_scratch[3:],
        width,
        HEAD_TILES,
        rank,
        row,
        early_plan(len(HEAD_TILES)),
    )
    late = Reduction(
        (late_source_ref, late_ref) + late_scratch[:3],
        late_scratch[3:],
        width + EXTRA,
        LATE_HEAD_TILES,
        rank,
        row,
    )
    mlp_kernel(
        early.reach,
        tokens_ref,
        cot_ref,
        att_ref,
        w_out_ref,
        gain_mlp_ref,
        w_gate_ref,
        w_up_ref,
        w_down_ref,
        out_ref,
        source_ref,
        rest_ref,
        gain_grad_ref,
        d_middle_ref,
        dot_ref,
        delta_ref,
    )
    back_kernel(
        ranks,
        None,
        (early, late, late_source_ref),
        tokens_ref,
        seg_ref,
        gain_attn_ref,
        wq_ref,
        wk_ref,
        wv_ref,
        table_ref,
        qt_ref,
        kv_ref,
        lse_ref,
        dot_ref,
        delta_ref,
        d_middle_ref,
        rest_ref,
        gain_grad_ref,
        d_inputs_ref,
        late_ref,
        turn_ref,
        *chain,
    )


def layer(
    ranks,
    tokens,
    seg_row,
    gain_attn,
    gain_mlp,
    wq,
    wk,
    wv,
    cot,
    w_out,
    w_gate,
    w_up,
    w_down,
):
    width, rows = tokens.shape
    hidden_units = w_gate.shape[1]
    vmem = pl.BlockSpec(memory_space=pltpu.VMEM)
    anywhere = pl.BlockSpec(memory_space=pl.ANY)
    dma = pltpu.SemaphoreType.DMA
    table = jnp.asarray(angle_table(ranks, rows))
    tiles = (3 * hidden_units + width) // LANES
    late_shape = (2 * TILES, width + EXTRA, LANES)
    scratch = [
        pltpu.VMEM((width, rows), bf16),
        pltpu.VMEM(w_out.shape, bf16),
        pltpu.VMEM(w_gate.shape, bf16),
        pltpu.VMEM(w_up.shape, bf16),
        pltpu.VMEM(w_down.shape, bf16),
        dma((5,)),
        pltpu.VMEM((HD, rows), f32),
        pltpu.VMEM((H, PAIR, rows), bf16),
        pltpu.VMEM((ranks, KVH, rows + META, PAIR), bf16),
        pltpu.VMEM((H * HD, rows), f32),
        pltpu.VMEM((16, rows), f32),
        pltpu.VMEM((16, rows), f32),
        pltpu.VMEM((16, rows), f32),
        dma(()),
        dma((ranks, KVH)),
        dma((ranks, KVH)),
        dma((ranks, KVH)),
        pltpu.VMEM((tiles, width, LANES), bf16),
        pltpu.VMEM((width, LANES), bf16),
        pltpu.VMEM((1, width), f32),
        pltpu.VMEM((width, rows), f32),
        pltpu.VMEM((H, PAIR, rows), bf16),
        pltpu.VMEM((16, rows), f32),
        pltpu.VMEM(late_shape, bf16),
    ]
    scratch += reduction_scratch(len(HEAD_TILES), width)
    scratch += reduction_scratch(1, width + EXTRA)
    scratch += back_scratch(ranks, rows, CROSSING)
    return pl.pallas_call(
        functools.partial(layer_kernel, ranks),
        out_shape=(
            jax.ShapeDtypeStruct((width, rows), bf16),
            jax.ShapeDtypeStruct((width, rows), f32),
            jax.ShapeDtypeStruct((tiles, width, LANES), bf16),
            jax.ShapeDtypeStruct(late_shape, bf16),
        ),
        in_specs=[vmem] * 7 + [anywhere] * 6,
        out_specs=(vmem,) * 4,
        scratch_shapes=scratch,
        compiler_params=pltpu.CompilerParams(
            collective_id=2, has_side_effects=True, vmem_limit_bytes=VMEM_LIMIT
        ),
        name="layer",
    )(
        tokens,
        seg_row,
        gain_attn,
        gain_mlp,
        wq,
        wk,
        wv,
        table,
        cot,
        w_out,
        w_gate,
        w_up,
        w_down,
    )


def finish_kernel(
    gate_ref,
    up_ref,
    down_ref,
    grads_ref,
    late_ref,
    d_inputs_ref,
    low_output_ref,
    gain_attn_ref,
    query_ref,
    key_ref,
    value_ref,
    out_ref,
    gain_mlp_ref,
    grad_gate_ref,
    grad_up_ref,
    grad_down_ref,
    d_tokens_ref,
    output_ref,
):
    width = query_ref.shape[0]
    d_tokens_ref[...] = d_inputs_ref[...]
    output_ref[...] = low_output_ref[...]
    for tile in range(gate_ref.shape[0]):
        part = slice(tile * LANES, (tile + 1) * LANES)
        grad_gate_ref[:, part] = gate_ref[tile].astype(f32)
        grad_up_ref[:, part] = up_ref[tile].astype(f32)
        grad_down_ref[:, part] = down_ref[tile].astype(f32)

    @pl.when(pl.program_id(0) == 0)
    def _():
        late = jnp.concatenate(
            [late_ref[tile, :width, :].astype(f32) for tile in range(2 * TILES)], axis=1
        )
        q_cols, k_cols = H * HD, KVH * HD
        used = q_cols + 2 * k_cols
        query_ref[...] = late[:, :q_cols]
        key_ref[...] = late[:, q_cols : q_cols + k_cols].T
        value_ref[...] = late[:, q_cols + k_cols : used].T
        whole = grads_ref.shape[0]
        for tile in range(whole):
            out_ref[:, tile * LANES : (tile + 1) * LANES] = grads_ref[tile].astype(f32)
        out_ref[:, whole * LANES :] = late[:, used : used + width - whole * LANES]
        extra = [
            late_ref[tile, width : width + 16, :].astype(f32)
            for tile in range(-(-width // LANES))
        ]
        extra = jnp.concatenate(extra, axis=1)
        gain_attn_ref[...] = extra[0, :width]
        gain_mlp_ref[...] = extra[1, :width]


def finish(grads, late, d_inputs, output, hidden_units):
    tiles = hidden_units // LANES
    steps = FINISH_STEPS
    width, rows = d_inputs.shape
    each = tiles // steps
    whole = width // LANES
    fixed = lambda shape: pl.BlockSpec(shape, lambda i: (0,) * len(shape))
    per = FF_CHUNK // LANES // each
    tile_at = lambda kind: pl.BlockSpec(
        (each, width, LANES), lambda i: ((3 * (i // per) + kind) * per + i % per, 0, 0)
    )
    strip = pl.BlockSpec((width // steps, rows), lambda i: (i, 0))
    k_cols = KVH * HD
    return pl.pallas_call(
        finish_kernel,
        grid=(steps,),
        out_shape=(
            jax.ShapeDtypeStruct((width,), f32),
            jax.ShapeDtypeStruct((width, H * HD), f32),
            jax.ShapeDtypeStruct((k_cols, width), f32),
            jax.ShapeDtypeStruct((k_cols, width), f32),
            jax.ShapeDtypeStruct((H * HD, width), f32),
            jax.ShapeDtypeStruct((width,), f32),
            jax.ShapeDtypeStruct((width, hidden_units), f32),
            jax.ShapeDtypeStruct((width, hidden_units), f32),
            jax.ShapeDtypeStruct((width, hidden_units), f32),
            jax.ShapeDtypeStruct((width, rows), f32),
            jax.ShapeDtypeStruct((width, rows), bf16),
        ),
        in_specs=[
            tile_at(0),
            tile_at(1),
            tile_at(2),
            pl.BlockSpec((whole, width, LANES), lambda i: (3 * tiles // whole, 0, 0)),
            fixed(late.shape),
            strip,
            strip,
        ],
        out_specs=(
            fixed((width,)),
            fixed((width, H * HD)),
            fixed((k_cols, width)),
            fixed((k_cols, width)),
            fixed((H * HD, width)),
            fixed((width,)),
        )
        + (pl.BlockSpec((width, each * LANES), lambda i: (0, i)),) * 3
        + (strip, strip),
        compiler_params=pltpu.CompilerParams(vmem_limit_bytes=VMEM_LIMIT),
        name="finish",
    )(grads, grads, grads, grads, late, d_inputs, output)


def local(
    ranks,
    batches,
    tokens,
    segment_ids,
    gain_attn,
    w_query,
    w_key,
    w_value,
    w_out,
    gain_mlp,
    w_gate,
    w_up,
    w_down,
    cotangent,
):
    tokens_t, cot_t = tokens[0].T, cotangent[0].T
    w_key_t, w_value_t, w_down_t = w_key.T, w_value.T, w_down.T
    if ranks == 2 * TILES and batches == 4:
        output, d_inputs, grads, late = layer(
            ranks,
            tokens_t,
            segment_ids,
            gain_attn,
            gain_mlp,
            w_query,
            w_key_t,
            w_value_t,
            cot_t,
            w_out,
            w_gate,
            w_up,
            w_down_t,
        )
    else:
        qt, kv, att, lse = attend(
            tokens_t, segment_ids, gain_attn, w_query, w_key_t, w_value_t, ranks
        )
        output, grads, rest, grad_gain_mlp, d_middle, dot_t, delta = mlp(
            tokens_t, cot_t, att, w_out, gain_mlp, w_gate, w_up, w_down_t
        )
        d_inputs, late = back(
            ranks,
            tokens_t,
            segment_ids,
            gain_attn,
            w_query,
            w_key_t,
            w_value_t,
            qt,
            kv,
            lse,
            dot_t,
            delta,
            d_middle,
            rest,
            grad_gain_mlp,
        )
        grads, late = lax.psum((grads, late), ("seq", "batch"))
    (
        grad_gain_attn,
        grad_query,
        grad_key,
        grad_value,
        grad_out,
        grad_gain_mlp,
        grad_gate,
        grad_up,
        grad_down,
        d_tokens,
        output,
    ) = finish(grads, late, d_inputs, output, w_gate.shape[1])
    return (
        output.T[None],
        d_tokens.T[None],
        grad_gain_attn,
        grad_query,
        grad_key.T,
        grad_value.T,
        grad_out,
        grad_gain_mlp,
        grad_gate,
        grad_up,
        grad_down.T,
    )


def solution(mesh):
    split = P("batch", "seq", None)
    return jax.shard_map(
        functools.partial(local, mesh.shape["seq"], mesh.shape["batch"]),
        mesh=mesh,
        in_specs=(split, P("batch", "seq")) + (P(),) * 9 + (split,),
        out_specs=(split, split) + (P(),) * 9,
        check_vma=False,
    )
```
